32 devices in a mesh: px: 4 (over z), py: 8 (over y, x, core).
Axes of the slice: x: 2, y: 2, z: 4, core: 2. Of those that a mesh axis runs over, the one named last changes fastest.
Arguments:
- a_blocks: bfloat16 [3072, 27, 4096], P(('px', 'py')), may hold values from -1.5 to 1.5
- p_blocks: bfloat16 [3072, 4096], P(('px', 'py')), may hold values from -0.75 to 0.75
- a_source: int32 [3072, 27], P(('px', 'py')), may hold values from 0 to 351, as said below
- send_list: int32 [32, 32, 8], P(('px', 'py')), may hold values from -1 to 95, as said below
- agg_local: int32 [3072], P(('px', 'py')), may hold values from 0 to 15, as said below
- coarse_slot: int32 [3072, 27], P(('px', 'py')), may hold values from 0 to 26
- coarse_target: int32 [512], P(('px', 'py')), may hold values from 0 to 511, as said below
Outputs:
- coarse: bfloat16 [512, 27, 4096], P(('px', 'py'))
The draws below stay inside these ranges and needn't reach their ends.
Inputs may be any that keep to these rules, and one draw needn't show every extreme that they name: `a_source`: column 0 of a row is the row itself. An entry of 96 or more names a slot received from device (entry - 96) // 8, slot (entry - 96) % 8, which that device fills; every filled slot is named by some entry of the receiving device. `send_list`: filled slots from one sender to one receiver come first; no device sends to itself; each device fills all 8 slots for the device after it in px+py order; row 95 is sent in every draw. `agg_local`: each of a device's 16 agglomerates holds exactly 6 of its elements. `coarse_target`: A permutation of the coarse rows; the rows formed on a device go to devices with the same px index; at most 2 go from one device to one device, and in every draw exactly 2 for each pair that is used.
All inputs are finite; a program needn't handle non-finite values.
Results may differ from the reference program's by a relative error of at most 0.0049.
Values may be sent and summed in bfloat16 or wider, within the bound.
No kernel may reach another device: no remote copies, remote signals or barrier semaphores. Data moves between devices by JAX's collectives and lax.ppermute only.
A program may use at most 384 MiB of HBM per device.

```python
import jax
import jax.numpy as jnp
from jax import lax

B = 64
NB = 96
K = 27
S = 27
AGG = 6
Q = 8
CCAP = 2
XDEV = 4
YDEV = 8
ALLDEV = 32
NCL = 16
ROWS = 3072
COARSE = 512


def ghost_pattern(key):
    count_key, row_key, ref_key = jax.random.split(jax.random.fold_in(key, 7), 3)
    counts = jax.random.randint(count_key, (ALLDEV, ALLDEV), 0, Q + 1)
    device_ids = jnp.arange(ALLDEV)
    counts = jnp.where(device_ids[:, None] == device_ids[None, :], 0, counts)
    following = (device_ids[:, None] + 1) % ALLDEV == device_ids[None, :]
    counts = jnp.where(following, Q, counts)
    slot_ids = jnp.arange(Q)
    filled = slot_ids[None, None, :] < counts[:, :, None]
    rows_sent = jax.random.randint(row_key, (ALLDEV, ALLDEV, Q), 0, NB)
    rows_sent = rows_sent.at[0, 1 % ALLDEV, 0].set(NB - 1)
    sending = jnp.where(filled, rows_sent, -1)
    positions = NB * (K - 1)

    def receiver(device):
        sub_key = jax.random.fold_in(ref_key, device)
        perm_key, pick_key, local_key, coin_key = jax.random.split(sub_key, 4)
        active = filled[:, device, :].reshape(-1)
        active_count = jnp.sum(active.astype(jnp.int32))
        slot_order = jnp.argsort(jnp.where(active, 0, 1), stable=True)
        turns = jnp.arange(positions)
        picked = jax.random.randint(pick_key, (positions,), 0, 1 << 30) % active_count
        any_slot = slot_order[picked]
        first_slot = slot_order[jnp.minimum(turns, ALLDEV * Q - 1)]
        local_rows = jax.random.randint(local_key, (positions,), 0, NB)
        coins = jax.random.randint(coin_key, (positions,), 0, 4)
        extra = jnp.where(coins == 0, NB + any_slot, local_rows)
        values = jnp.where(turns < active_count, NB + first_slot, extra)
        places = jax.random.permutation(perm_key, positions)
        refs = jnp.zeros((positions,), jnp.int32).at[places].set(values.astype(jnp.int32))
        own = jnp.arange(NB, dtype=jnp.int32)[:, None]
        return jnp.concatenate([own, refs.reshape(NB, K - 1)], axis=1)
    sources = jax.vmap(receiver)(jnp.arange(ALLDEV))
    return (sending.astype(jnp.int32), sources.reshape(ALLDEV * NB, K).astype(jnp.int32))


def draw_a_source(key, part):
    return ghost_pattern(key)[1]


def draw_send_list(key, part):
    return ghost_pattern(key)[0]


def draw_agg_local(key, part):

    def one_device(device):
        return jax.random.permutation(jax.random.fold_in(key, device), NB) // AGG
    return jax.vmap(one_device)(jnp.arange(ALLDEV)).reshape(-1).astype(jnp.int32)


def draw_coarse_target(key, part):
    shift_key, order_key = jax.random.split(jax.random.fold_in(key, 11))
    used = NCL // CCAP

    def group(xrow):
        shifts = jax.random.permutation(jax.random.fold_in(shift_key, xrow), YDEV)[:used]

        def source(ypos):
            local = jnp.arange(NCL)
            unit = local // CCAP
            within = local % CCAP
            dest_y = (ypos + shifts[unit]) % YDEV
            target = (xrow * YDEV + dest_y) * NCL + unit * CCAP + within
            order = jax.random.permutation(jax.random.fold_in(order_key, xrow * YDEV + ypos), NCL)
            return target[order]
        return jax.vmap(source)(jnp.arange(YDEV))
    return jax.vmap(group)(jnp.arange(XDEV)).reshape(-1).astype(jnp.int32)


def with_ends(values, stream_key, low, largest):
    longest = values.shape.index(max(values.shape))
    spots = []
    for shift in (0, 1):
        where = [jax.random.randint(jax.random.fold_in(stream_key, axis), (), 0, length) for axis, length in enumerate(values.shape)]
        where[longest] = (where[longest] + shift) % values.shape[longest]
        spots.append(tuple(where))
    return values.at[spots[0]].set(low).at[spots[1]].set(largest)


def level_of(stream_key, extent, cuts, smallest, high):
    def one(position, parts):
        steps = jax.random.uniform(jax.random.fold_in(jax.random.fold_in(stream_key, 6), position), (parts,), jnp.float32, smallest / len(cuts), high / len(cuts))
        return jnp.repeat(jnp.exp(steps), extent[position] // parts).reshape((-1,) + (1,) * (len(extent) - position - 1))

    level = one(*cuts[0])
    for cut in cuts[1:]:
        level = level * one(*cut)
    return level


def gaussian(key, shape, width, limit, shards=(), held_as=jnp.bfloat16):
    factor_of = level_of(key, shape, shards, -0.22, 0.18) if shards else 1.0
    entries = jax.random.normal(key, shape, jnp.float32) * width * factor_of
    return jnp.minimum(jnp.maximum(entries, -limit), limit).astype(held_as)


def setup_inputs(seed: int = 0) -> dict:
    splits = jax.random.split(jax.random.key(seed), 8)
    return {
        "a_blocks": gaussian(splits[0], (ROWS, K, B * B), 0.25, 1.5, ((0, 32),)),
        "p_blocks": gaussian(splits[1], (ROWS, B * B), B ** -0.5, 0.75, ((0, 32),)),
        "a_source": draw_a_source(jax.random.fold_in(splits[7], 71), 0),
        "send_list": draw_send_list(jax.random.fold_in(splits[7], 71), 0),
        "agg_local": draw_agg_local(jax.random.fold_in(splits[7], 71), 0),
        "coarse_slot": with_ends(jax.random.randint(splits[5], (ROWS, K), 0, S), jax.random.fold_in(splits[5], 1), 0, S - 1).astype(jnp.int32),
        "coarse_target": draw_coarse_target(jax.random.fold_in(splits[7], 71), 0),
    }


def reference(a_blocks, p_blocks, a_source, send_list, agg_local, coarse_slot, coarse_target):
    flat_size = B * B

    def one_device(device):
        start = device * NB
        a_rows = lax.dynamic_slice_in_dim(a_blocks, start, NB, 0)
        p_rows = lax.dynamic_slice_in_dim(p_blocks, start, NB, 0)
        sources = lax.dynamic_slice_in_dim(a_source, start, NB, 0)
        groups = lax.dynamic_slice_in_dim(agg_local, start, NB, 0)
        slots = lax.dynamic_slice_in_dim(coarse_slot, start, NB, 0)
        ghost = jnp.maximum(sources - NB, 0)
        sender = (ghost // Q).astype(jnp.int32)
        slot_in = (ghost % Q).astype(jnp.int32)
        sent_row = send_list[sender, device, slot_in]
        is_local = sources < NB
        global_row = jnp.where(is_local, start + sources, sender * NB + sent_row)
        filled = is_local | (sent_row >= 0)
        columns = p_blocks[jnp.maximum(global_row, 0).astype(jnp.int32)]
        columns = jnp.where(filled[:, :, None], columns, jnp.zeros_like(columns))
        a_split = a_rows.reshape(NB, K, B, B).astype(jnp.float32)
        col_split = columns.reshape(NB, K, B, B).astype(jnp.float32)
        product = jnp.einsum("gkij,gkjl->gkil", a_split, col_split).astype(jnp.bfloat16)
        own_split = p_rows.reshape(NB, B, B).astype(jnp.float32)
        triple = jnp.einsum("gia,gkil->gkal", own_split, product.astype(jnp.float32))
        segment_ids = (groups[:, None] * S + slots).reshape(-1).astype(jnp.int32)
        summed = jax.ops.segment_sum(triple.reshape(NB * K, flat_size), segment_ids, num_segments=NCL * S)
        return summed.astype(jnp.bfloat16).reshape(NCL, S, flat_size)

    partials = lax.map(one_device, jnp.arange(ALLDEV, dtype=jnp.int32))
    flat_rows = partials.reshape(COARSE, S, flat_size)
    result = jnp.zeros_like(flat_rows).at[coarse_target.astype(jnp.int32)].set(flat_rows)
    return result
```

```python
import jax
import jax.numpy as jnp
from jax import lax
from jax.experimental import pallas as pl
from jax.experimental.pallas import tpu as pltpu
from jax.sharding import PartitionSpec as P

B = 64
FLAT = B * B
LANES = 128
HALF = B // 2
S = 27
AGG = 6
CCAP = 2
GROUP = 8
TILES = FLAT // LANES
KROWS = GROUP * TILES
MIB = 1 << 20


def lane_low(rows):
    return lax.broadcasted_iota(jnp.int32, (rows, LANES), 1) < B


def swap_halves(x):
    return pltpu.roll(x, B, 1)


def as_tiles(x):
    lead, rows = x.shape[:-2], x.shape[-2]
    split = x.reshape(*lead, rows // GROUP, GROUP, TILES, LANES)
    return jnp.swapaxes(split, -3, -2).reshape(*lead, rows // GROUP, KROWS, LANES)


def from_tiles(x):
    lead, groups = x.shape[:-3], x.shape[-3]
    split = x.reshape(*lead, groups, TILES, GROUP, LANES)
    return jnp.swapaxes(split, -3, -2).reshape(*lead, groups * GROUP, FLAT)


def block_perm(transposed):
    block_axis, tile_axis = (1, 0) if transposed else (0, 1)
    shape = (KROWS, KROWS)
    block_row = lax.broadcasted_iota(jnp.int32, shape, block_axis)
    tile_row = lax.broadcasted_iota(jnp.int32, shape, tile_axis)
    same_r = (block_row // HALF) == (tile_row % GROUP)
    want = 2 * ((tile_row % LANES) // GROUP) + tile_row // LANES
    same_j = (block_row % HALF) == want
    return jnp.where(same_r & same_j, 1.0, 0.0).astype(jnp.bfloat16)


def pack_kernel(send_ref, p_ref, out_ref, own_ref, table_ref):
    groups = p_ref.shape[0]
    rows = groups * GROUP
    slots, peers = send_ref.shape
    perm = block_perm(False)
    low = lane_low(LANES)

    def to_blocks(g):
        top, bottom = p_ref[g, 0:LANES, :], p_ref[g, LANES:KROWS, :]
        even = jnp.where(low, top, swap_halves(bottom))
        odd = jnp.where(low, swap_halves(top), bottom)
        return jnp.concatenate([even, odd], axis=0)

    for g in range(0, groups, 2):
        both = jnp.concatenate([to_blocks(g), to_blocks(g + 1)], axis=1)
        blocks = jnp.dot(perm, both, preferred_element_type=jnp.float32).astype(jnp.bfloat16)
        for h in range(2):
            piece = blocks[:, h * LANES : (h + 1) * LANES].reshape(GROUP, HALF, LANES)
            table_ref[pl.ds((g + h) * GROUP, GROUP)] = piece
    table_ref[rows] = jnp.zeros((HALF, LANES), jnp.bfloat16)
    own_ref[...] = table_ref[0:rows]

    def fill(peer, carry):
        for slot in range(slots):
            wanted = send_ref[slot, peer]
            out_ref[peer * slots + slot] = table_ref[jnp.where(wanted < 0, rows, wanted)]
        return carry

    lax.fori_loop(0, peers, fill, 0)


def project_kernel(a_ref, p_ref, out_ref, left_ref):
    per_row = a_ref.shape[0]
    pairs = out_ref.shape[2]
    flipped = p_ref[0].T
    row_of = lax.broadcasted_iota(jnp.int32, (B, KROWS), 1) % GROUP
    zero = jnp.zeros((B, KROWS), jnp.bfloat16)
    for r in range(GROUP):
        mine = row_of == r
        left_ref[r * B : (r + 1) * B, 0:KROWS] = jnp.where(mine, flipped[0:B], zero)
        left_ref[r * B : (r + 1) * B, KROWS:] = jnp.where(mine, flipped[B:], zero)
    low = lane_low(KROWS)

    def pair_of(pair):
        first = a_ref[2 * pair, 0]
        second = a_ref[min(2 * pair + 1, per_row - 1), 0]
        even = jnp.where(low, first, swap_halves(second))
        odd = jnp.where(low, swap_halves(first), second)
        return jnp.concatenate([even, odd], axis=0)

    for pair in range(0, pairs, 2):
        right = jnp.concatenate([pair_of(pair), pair_of(pair + 1)], axis=1)
        both = jnp.dot(left_ref[...], right, preferred_element_type=jnp.float32).astype(jnp.bfloat16)
        for h in range(2):
            out_ref[0, :, pair + h] = both[:, h * LANES : (h + 1) * LANES].reshape(GROUP, B, LANES)


def combine_kernel(
    source_ref, slot_ref, agg_ref, target_ref, t_ref, own_ref, ghost_ref, out_ref,
    table_ref, even_ref, odd_ref, bucket_ref, place_ref, count_ref,
):
    step = pl.program_id(0)
    per_row, rows = source_ref.shape
    ghosts = ghost_ref.shape[0]
    coarse_here = target_ref.shape[0]
    peers = out_ref.shape[0]
    pairs = t_ref.shape[2]
    low = lane_low(HALF)
    zero_half = jnp.zeros((HALF, LANES), jnp.bfloat16)
    nothing, unused = rows + ghosts, coarse_here * S

    @pl.when(step == 0)
    def _():
        def expand(ref, base):
            def one(i, carry):
                block = ref[i]
                turned = swap_halves(block)
                table_ref[base + i, 0:HALF] = jnp.where(low, block, turned)
                table_ref[base + i, HALF:] = jnp.where(low, turned, block)
                return carry

            lax.fori_loop(0, ref.shape[0], one, 0, unroll=8)

        expand(own_ref, 0)
        expand(ghost_ref, rows)
        table_ref[nothing] = jnp.zeros((B, LANES), jnp.bfloat16)

        def clear(i, carry):
            even_ref[i] = jnp.zeros((HALF, LANES), jnp.float32)
            odd_ref[i] = jnp.zeros((HALF, LANES), jnp.float32)
            return carry

        lax.fori_loop(0, unused, clear, 0, unroll=8)

    low_all = lane_low(B)
    zero_all = jnp.zeros((B, LANES), jnp.bfloat16)

    def one_row(r, carry):
        row = step * GROUP + r
        base = agg_ref[row] * S
        for pair in range(pairs):
            k0, k1 = 2 * pair, 2 * pair + 1
            first = jnp.where(low_all, table_ref[source_ref[k0, row]], zero_all)
            if k1 < per_row:
                second = jnp.where(low_all, zero_all, table_ref[source_ref[k1, row]])
            else:
                second = zero_all
            weights = jnp.concatenate([first, second], axis=0)
            value = jnp.dot(t_ref[0, r, pair], weights, preferred_element_type=jnp.float32)
            top, bottom = value[0:HALF], value[HALF:]
            to0 = base + slot_ref[k0, row]
            even_ref[to0] += jnp.where(low, top, swap_halves(bottom))
            if k1 < per_row:
                to1 = base + slot_ref[k1, row]
                odd_ref[to1] += jnp.where(low, swap_halves(top), bottom)
        return carry

    lax.fori_loop(0, GROUP, one_row, 0)

    @pl.when(step == pl.num_programs(0) - 1)
    def _():
        for p in range(peers):
            count_ref[p] = 0
            for q in range(CCAP):
                place_ref[p * CCAP + q] = -1

        def assign(c, carry):
            target = target_ref[c]
            peer = target // coarse_here % peers
            bucket = peer * CCAP + count_ref[peer]
            count_ref[peer] = count_ref[peer] + 1
            bucket_ref[c] = bucket
            place_ref[bucket] = target % coarse_here
            return carry

        lax.fori_loop(0, coarse_here, assign, 0)
        payload = CCAP * S * HALF
        second_slot = lax.broadcasted_iota(jnp.int32, (out_ref.shape[1] - payload, LANES), 1) // HALF % CCAP

        def note(p, carry):
            value = jnp.full(second_slot.shape, -1, jnp.int32)
            for q in range(CCAP):
                value = jnp.where(second_slot == q, place_ref[p * CCAP + q], value)
            out_ref[p, payload:] = value.astype(jnp.float32).astype(jnp.bfloat16)
            return carry

        lax.fori_loop(0, peers, note, 0)

        def finish(c, carry):
            bucket = bucket_ref[c]
            peer = bucket // CCAP
            start = bucket % CCAP * (S * HALF)
            for s in range(S):
                total = even_ref[c * S + s] + odd_ref[c * S + s]
                here = pl.multiple_of(start + s * HALF, HALF)
                out_ref[peer, pl.ds(here, HALF)] = total.astype(jnp.bfloat16)
            return carry

        lax.fori_loop(0, coarse_here, finish, 0)


def place_kernel(in_ref, out_ref, from_ref):
    step = pl.program_id(0)
    peers = in_ref.shape[0]
    per_step, groups = out_ref.shape[0], out_ref.shape[1]
    payload = CCAP * S * HALF

    @pl.when(step == 0)
    def _():
        for p in range(peers):
            notes = in_ref[p, payload:].astype(jnp.float32)
            which = lax.broadcasted_iota(jnp.int32, notes.shape, 1) // HALF
            for q in range(CCAP):
                place = jnp.max(jnp.where(which == q, notes, -1.0)).astype(jnp.int32)

                @pl.when(place >= 0)
                def _():
                    from_ref[place] = p * CCAP + q

    perm = block_perm(True)
    low = lane_low(LANES)
    for i in range(per_step):
        s = step * per_step + i
        columns = []
        for g in range(groups):
            blocks = []
            for c in range(GROUP):
                bucket = from_ref[g * GROUP + c]
                here = pl.multiple_of((bucket % CCAP * S + s) * HALF, HALF)
                blocks.append(in_ref[bucket // CCAP, pl.ds(here, HALF)])
            columns.append(jnp.concatenate(blocks, axis=0))
        moved = jnp.dot(perm, jnp.concatenate(columns, axis=1), preferred_element_type=jnp.float32)
        moved = moved.astype(jnp.bfloat16)
        for g in range(groups):
            mine = moved[:, g * LANES : (g + 1) * LANES]
            even, odd = mine[0:LANES], mine[LANES:]
            out_ref[i, g, 0:LANES] = jnp.where(low, even, swap_halves(odd))
            out_ref[i, g, LANES:] = jnp.where(low, swap_halves(even), odd)


def whole(shape):
    return pl.BlockSpec(shape, lambda *_: (0,) * len(shape))


def body(a_blocks, p_blocks, a_source, send_list, agg_local, coarse_slot, coarse_target):
    rows, per_row, _ = a_blocks.shape
    peers = lax.axis_size(("px", "py"))
    peers_y = lax.axis_size("py")
    slots = send_list.shape[2]
    coarse_here = rows // AGG
    groups = rows // GROUP
    pairs = (per_row + 3) // 4 * 2
    bf16 = jnp.bfloat16
    smem = pl.BlockSpec(memory_space=pltpu.SMEM)

    a_tiles = as_tiles(a_blocks.transpose(1, 0, 2))
    p_tiles = as_tiles(p_blocks)
    outgoing, own = pl.pallas_call(
        pack_kernel,
        in_specs=[smem, whole((groups, KROWS, LANES))],
        out_specs=[whole((peers * slots, HALF, LANES)), whole((rows, HALF, LANES))],
        out_shape=[
            jax.ShapeDtypeStruct((peers * slots, HALF, LANES), bf16),
            jax.ShapeDtypeStruct((rows, HALF, LANES), bf16),
        ],
        scratch_shapes=[pltpu.VMEM((rows + 1, HALF, LANES), bf16)],
        compiler_params=pltpu.CompilerParams(vmem_limit_bytes=24 * MIB),
    )(send_list[0].T, p_tiles)
    arrived = lax.all_to_all(
        outgoing.reshape(peers, slots, HALF, LANES), ("px", "py"), split_axis=0, concat_axis=0, tiled=True
    ).reshape(peers * slots, HALF, LANES)

    projected = pl.pallas_call(
        project_kernel,
        grid=(groups,),
        in_specs=[
            pl.BlockSpec((per_row, 1, KROWS, LANES), lambda g: (0, g, 0, 0)),
            pl.BlockSpec((1, KROWS, LANES), lambda g: (g, 0, 0)),
        ],
        out_specs=pl.BlockSpec((1, GROUP, pairs, B, LANES), lambda g: (g, 0, 0, 0, 0)),
        out_shape=jax.ShapeDtypeStruct((groups, GROUP, pairs, B, LANES), bf16),
        scratch_shapes=[pltpu.VMEM((GROUP * B, 2 * KROWS), bf16)],
        compiler_params=pltpu.CompilerParams(vmem_limit_bytes=40 * MIB),
        cost_estimate=pl.CostEstimate(
            flops=2 * 512 * 512 * 128 * pairs * groups, bytes_accessed=45_000_000, transcendentals=0
        ),
    )(a_tiles, p_tiles)

    sums = coarse_here * S
    coarse_rows = CCAP * S * HALF + 16
    sent = pl.pallas_call(
        combine_kernel,
        grid=(groups,),
        in_specs=[
            smem, smem, smem, smem,
            pl.BlockSpec((1, GROUP, pairs, B, LANES), lambda g: (g, 0, 0, 0, 0)),
            whole((rows, HALF, LANES)),
            whole((peers * slots, HALF, LANES)),
        ],
        out_specs=whole((peers_y, coarse_rows, LANES)),
        out_shape=jax.ShapeDtypeStruct((peers_y, coarse_rows, LANES), bf16),
        scratch_shapes=[
            pltpu.VMEM((rows + peers * slots + 1, B, LANES), bf16),
            pltpu.VMEM((sums, HALF, LANES), jnp.float32),
            pltpu.VMEM((sums, HALF, LANES), jnp.float32),
            pltpu.SMEM((coarse_here,), jnp.int32),
            pltpu.SMEM((peers_y * CCAP,), jnp.int32),
            pltpu.SMEM((peers_y,), jnp.int32),
        ],
        compiler_params=pltpu.CompilerParams(vmem_limit_bytes=60 * MIB),
    )(a_source.T, coarse_slot.T, agg_local, coarse_target, projected, own, arrived)

    received = lax.all_to_all(sent, "py", split_axis=0, concat_axis=0, tiled=True)

    per_step = 3
    out_groups = coarse_here // GROUP
    placed = pl.pallas_call(
        place_kernel,
        grid=(S // per_step,),
        in_specs=[whole((peers_y, coarse_rows, LANES))],
        out_specs=pl.BlockSpec((per_step, out_groups, KROWS, LANES), lambda s: (s, 0, 0, 0)),
        out_shape=jax.ShapeDtypeStruct((S, out_groups, KROWS, LANES), bf16),
        scratch_shapes=[pltpu.SMEM((coarse_here,), jnp.int32)],
        compiler_params=pltpu.CompilerParams(vmem_limit_bytes=24 * MIB),
    )(received)
    return from_tiles(placed).transpose(1, 0, 2)


def solution(mesh):
    rows = ("px", "py")
    in_specs = (
        P(rows, None, None),
        P(rows, None),
        P(rows, None),
        P(rows, None, None),
        P(rows),
        P(rows, None),
        P(rows),
    )
    return jax.shard_map(body, mesh=mesh, in_specs=in_specs, out_specs=P(rows, None, None), check_vma=False)
```

```python
import functools

import jax
import jax.numpy as jnp
from jax import lax
from jax.experimental import pallas as pl
from jax.experimental.pallas import tpu as pltpu
from jax.sharding import PartitionSpec as P

B = 64
FLAT = B * B
LANES = 128
HALF = B // 2
S = 27
AGG = 6
CCAP = 2
GROUP = 8
TILES = FLAT // LANES
KROWS = GROUP * TILES
CHUNK = 16
RING = 4
MIB = 1 << 20


def lane_low(rows):
    return lax.broadcasted_iota(jnp.int32, (rows, LANES), 1) < B


def swap_halves(x):
    return pltpu.roll(x, B, 1)


def as_tiles(x):
    lead, rows = x.shape[:-2], x.shape[-2]
    split = x.reshape(*lead, rows // GROUP, GROUP, TILES, LANES)
    return jnp.swapaxes(split, -3, -2).reshape(*lead, rows // GROUP, KROWS, LANES)


def from_tiles(x):
    lead, groups = x.shape[:-3], x.shape[-3]
    split = x.reshape(*lead, groups, TILES, GROUP, LANES)
    return jnp.swapaxes(split, -3, -2).reshape(*lead, groups * GROUP, FLAT)


def block_perm(transposed):
    block_axis, tile_axis = (1, 0) if transposed else (0, 1)
    shape = (KROWS, KROWS)
    block_row = lax.broadcasted_iota(jnp.int32, shape, block_axis)
    tile_row = lax.broadcasted_iota(jnp.int32, shape, tile_axis)
    same_r = (block_row // HALF) == (tile_row % GROUP)
    want = 2 * ((tile_row % LANES) // GROUP) + tile_row // LANES
    same_j = (block_row % HALF) == want
    return jnp.where(same_r & same_j, 1.0, 0.0).astype(jnp.bfloat16)


def pack_kernel(send_ref, p_ref, out_ref, own_ref, table_ref):
    groups = p_ref.shape[0]
    rows = groups * GROUP
    slots, peers = send_ref.shape
    perm = block_perm(False)
    low = lane_low(LANES)

    def to_blocks(g):
        top, bottom = p_ref[g, 0:LANES, :], p_ref[g, LANES:KROWS, :]
        even = jnp.where(low, top, swap_halves(bottom))
        odd = jnp.where(low, swap_halves(top), bottom)
        return jnp.concatenate([even, odd], axis=0)

    for g in range(0, groups, 2):
        both = jnp.concatenate([to_blocks(g), to_blocks(g + 1)], axis=1)
        blocks = jnp.dot(perm, both, preferred_element_type=jnp.float32).astype(jnp.bfloat16)
        for h in range(2):
            piece = blocks[:, h * LANES : (h + 1) * LANES].reshape(GROUP, HALF, LANES)
            table_ref[pl.ds((g + h) * GROUP, GROUP)] = piece
    table_ref[rows] = jnp.zeros((HALF, LANES), jnp.bfloat16)
    own_ref[...] = table_ref[0:rows]

    def fill(peer, carry):
        for slot in range(slots):
            wanted = send_ref[slot, peer]
            out_ref[peer * slots + slot] = table_ref[jnp.where(wanted < 0, rows, wanted)]
        return carry

    lax.fori_loop(0, peers, fill, 0)


def fold(value, low):
    top, bottom = value[0:HALF], value[HALF:]
    return jnp.where(low, top, swap_halves(bottom)), jnp.where(low, swap_halves(top), bottom)


def project_kernel(
    ghosts, source_ref, slot_ref, agg_ref, a_ref, p_ref, own_ref, sum_ref, tiles_hbm, meta_ref, count_ref,
    left_ref, first_ref, second_ref, odd_ref, even_tiles, odd_tiles, merged_ref, done_ref, sems,
):
    step = pl.program_id(0)
    per_row, rows = source_ref.shape
    pairs = (per_row + 3) // 4 * 2
    unused = sum_ref.shape[0]
    low_half, low_all = lane_low(HALF), lane_low(B)
    zero_all = jnp.zeros((B, LANES), jnp.bfloat16)

    @pl.when(step == 0)
    def _():
        done_ref[0] = 0

        def expand(i, carry):
            block = own_ref[i]
            turned = swap_halves(block)
            zero = jnp.zeros((HALF, LANES), jnp.bfloat16)
            first_ref[i, 0:HALF] = jnp.where(low_half, block, zero)
            first_ref[i, HALF:] = jnp.where(low_half, turned, zero)
            second_ref[i, 0:HALF] = jnp.where(low_half, zero, turned)
            second_ref[i, HALF:] = jnp.where(low_half, zero, block)
            return carry

        lax.fori_loop(0, rows, expand, 0, unroll=8)
        first_ref[rows] = zero_all
        second_ref[rows] = zero_all

        def clear(i, carry):
            sum_ref[i] = jnp.zeros((HALF, LANES), jnp.float32)
            odd_ref[i] = jnp.zeros((HALF, LANES), jnp.float32)
            return carry

        lax.fori_loop(0, unused, clear, 0, unroll=8)

    flipped = p_ref[0].T
    row_of = lax.broadcasted_iota(jnp.int32, (B, KROWS), 1) % GROUP
    zero = jnp.zeros((B, KROWS), jnp.bfloat16)
    for r in range(GROUP):
        mine = row_of == r
        left_ref[r * B : (r + 1) * B, 0:KROWS] = jnp.where(mine, flipped[0:B], zero)
        left_ref[r * B : (r + 1) * B, KROWS:] = jnp.where(mine, flipped[B:], zero)
    low = lane_low(KROWS)

    def pair_of(pair):
        first = a_ref[2 * pair, 0]
        second = a_ref[min(2 * pair + 1, per_row - 1), 0]
        even = jnp.where(low, first, swap_halves(second))
        odd = jnp.where(low, swap_halves(first), second)
        return jnp.concatenate([even, odd], axis=0)

    before = done_ref[0]
    even_count = jnp.int32(0)
    odd_count = jnp.int32(0)
    for pair in range(0, pairs, 2):
        right = jnp.concatenate([pair_of(pair), pair_of(pair + 1)], axis=1)
        both = jnp.dot(left_ref[...], right, preferred_element_type=jnp.float32).astype(jnp.bfloat16)
        for r in range(GROUP):
            row = step * GROUP + r
            base = agg_ref[row] * S
            moving = both[r * B : (r + 1) * B]
            weights, targets = [], []
            for h in range(2):
                tile = moving[:, h * LANES : (h + 1) * LANES]
                k0, k1 = 2 * (pair + h), 2 * (pair + h) + 1
                source = source_ref[k0, row]
                target = base + slot_ref[k0, row]
                upper = first_ref[jnp.minimum(source, rows)]
                targets.append(target)
                if k0 > 0:
                    even_tiles[even_count] = tile
                    meta_ref[0, before + even_count] = jnp.maximum(source - rows, 0) * 1024 + target
                    even_count += (source >= rows).astype(jnp.int32)
                if k1 < per_row:
                    source = source_ref[k1, row]
                    target = base + slot_ref[k1, row]
                    lower = second_ref[jnp.minimum(source, rows)]
                    targets.append(target)
                    odd_tiles[odd_count] = tile
                    meta_ref[1, before + odd_count] = jnp.maximum(source - rows, 0) * 1024 + target
                    odd_count += (source >= rows).astype(jnp.int32)
                else:
                    lower = zero_all
                    targets.append(None)
                filled = jnp.concatenate([upper, lower], axis=0)
                blank = jnp.zeros_like(filled)
                weights.append(jnp.concatenate([filled, blank] if h == 0 else [blank, filled], axis=1))
            value = jnp.dot(moving, jnp.concatenate(weights, axis=0), preferred_element_type=jnp.float32)
            for h in range(2):
                even, odd = fold(value[:, h * LANES : (h + 1) * LANES], low_half)
                sum_ref[targets[2 * h]] += even
                if targets[2 * h + 1] is not None:
                    odd_ref[targets[2 * h + 1]] += odd

    after = jnp.maximum(even_count, odd_count)
    no_entry = ghosts * 1024 + unused

    def merge(i, carry):
        keep_even = jnp.where(low_all, i, after) < even_count
        keep_odd = jnp.where(low_all, after, i) < odd_count
        tile = jnp.where(keep_even, even_tiles[i], zero_all)
        merged_ref[before + i] = jnp.where(keep_odd, odd_tiles[i], tile)
        meta_ref[0, before + i] = jnp.where(i < even_count, meta_ref[0, before + i], no_entry)
        meta_ref[1, before + i] = jnp.where(i < odd_count, meta_ref[1, before + i], no_entry)
        return carry

    lax.fori_loop(0, after, merge, 0)
    done_ref[0] = before + after

    @pl.when(step == pl.num_programs(0) - 1)
    def _():
        def total(i, carry):
            sum_ref[i] += odd_ref[i]
            return carry

        lax.fori_loop(0, unused, total, 0, unroll=8)
        found = before + after
        chunks = (found + CHUNK - 1) // CHUNK

        def pad(i, carry):
            merged_ref[i] = zero_all
            meta_ref[0, i] = no_entry
            meta_ref[1, i] = no_entry
            return carry

        lax.fori_loop(found, chunks * CHUNK, pad, 0)
        count_ref[0] = chunks

        def copy(i):
            span = pl.ds(i * CHUNK, CHUNK)
            return pltpu.make_async_copy(merged_ref.at[span], tiles_hbm.at[span], sems.at[i % RING])

        def send(i, carry):
            @pl.when(i >= RING)
            def _():
                copy(i - RING).wait()

            copy(i).start()
            return carry

        lax.fori_loop(0, chunks, send, 0)
        lax.fori_loop(jnp.maximum(chunks - RING, 0), chunks, lambda i, c: (copy(i).wait(), c)[1], 0)


def combine_kernel(
    meta_ref, count_ref, target_ref, ghost_ref, sum_hbm, tiles_hbm, out_ref,
    table_ref, even_ref, odd_ref, tiles_ref, bucket_ref, place_ref, per_peer_ref, sum_sem, sems,
):
    ghosts = ghost_ref.shape[0]
    coarse_here = target_ref.shape[0]
    unused = coarse_here * S
    peers = out_ref.shape[0]
    chunks = count_ref[0]
    low_half, low_all = lane_low(HALF), lane_low(B)
    zero_all = jnp.zeros((B, LANES), jnp.bfloat16)
    load_sums = pltpu.make_async_copy(sum_hbm, even_ref.at[pl.ds(0, unused)], sum_sem)
    load_sums.start()

    def fetch(i):
        slot = i % RING
        return pltpu.make_async_copy(tiles_hbm.at[pl.ds(i * CHUNK, CHUNK)], tiles_ref.at[slot], sems.at[slot])

    for i in range(RING - 1):

        @pl.when(i < chunks)
        def _():
            fetch(i).start()

    def expand(i, carry):
        block = ghost_ref[i]
        turned = swap_halves(block)
        table_ref[i, 0:HALF] = jnp.where(low_half, block, turned)
        table_ref[i, HALF:] = jnp.where(low_half, turned, block)
        return carry

    lax.fori_loop(0, ghosts, expand, 0, unroll=8)
    table_ref[ghosts] = zero_all

    def clear(i, carry):
        odd_ref[i] = jnp.zeros((HALF, LANES), jnp.float32)
        return carry

    lax.fori_loop(0, unused, clear, 0, unroll=8)

    for p in range(peers):
        per_peer_ref[p] = 0
        for q in range(CCAP):
            place_ref[p * CCAP + q] = -1

    def assign(c, carry):
        target = target_ref[c]
        peer = target // coarse_here % peers
        bucket = peer * CCAP + per_peer_ref[peer]
        per_peer_ref[peer] = per_peer_ref[peer] + 1
        bucket_ref[c] = bucket
        place_ref[bucket] = target % coarse_here
        return carry

    lax.fori_loop(0, coarse_here, assign, 0)
    payload = CCAP * S * HALF
    second_slot = lax.broadcasted_iota(jnp.int32, (out_ref.shape[1] - payload, LANES), 1) // HALF % CCAP

    def note(p, carry):
        value = jnp.full(second_slot.shape, -1, jnp.int32)
        for q in range(CCAP):
            value = jnp.where(second_slot == q, place_ref[p * CCAP + q], value)
        out_ref[p, payload:] = value.astype(jnp.float32).astype(jnp.bfloat16)
        return carry

    lax.fori_loop(0, peers, note, 0)
    load_sums.wait()

    def work(i, carry):
        @pl.when(i + RING - 1 < chunks)
        def _():
            fetch(i + RING - 1).start()

        fetch(i).wait()
        slot = i % RING
        for j in range(0, CHUNK, 2):
            weights, targets = [], []
            for h in range(2):
                at = i * CHUNK + j + h
                even, odd = meta_ref[0, at], meta_ref[1, at]
                upper = jnp.where(low_all, table_ref[even // 1024], zero_all)
                lower = jnp.where(low_all, zero_all, table_ref[odd // 1024])
                targets += [even % 1024, odd % 1024]
                filled = jnp.concatenate([upper, lower], axis=0)
                blank = jnp.zeros_like(filled)
                weights.append(jnp.concatenate([filled, blank] if h == 0 else [blank, filled], axis=1))
            moving = jnp.concatenate([tiles_ref[slot, j], tiles_ref[slot, j + 1]], axis=1)
            value = jnp.dot(moving, jnp.concatenate(weights, axis=0), preferred_element_type=jnp.float32)
            for h in range(2):
                even, odd = fold(value[:, h * LANES : (h + 1) * LANES], low_half)
                even_ref[targets[2 * h]] += even
                odd_ref[targets[2 * h + 1]] += odd
        return carry

    lax.fori_loop(0, chunks, work, 0)

    def finish(c, carry):
        bucket = bucket_ref[c]
        start = bucket % CCAP * (S * HALF)
        for s in range(S):
            total = even_ref[c * S + s] + odd_ref[c * S + s]
            here = pl.multiple_of(start + s * HALF, HALF)
            out_ref[bucket // CCAP, pl.ds(here, HALF)] = total.astype(jnp.bfloat16)
        return carry

    lax.fori_loop(0, coarse_here, finish, 0)


def place_kernel(in_ref, out_ref, from_ref):
    step = pl.program_id(0)
    peers = in_ref.shape[0]
    per_step, groups = out_ref.shape[0], out_ref.shape[1]
    payload = CCAP * S * HALF

    @pl.when(step == 0)
    def _():
        for p in range(peers):
            notes = in_ref[p, payload:].astype(jnp.float32)
            which = lax.broadcasted_iota(jnp.int32, notes.shape, 1) // HALF
            for q in range(CCAP):
                place = jnp.max(jnp.where(which == q, notes, -1.0)).astype(jnp.int32)

                @pl.when(place >= 0)
                def _():
                    from_ref[place] = p * CCAP + q

    perm = block_perm(True)
    low = lane_low(LANES)
    for i in range(per_step):
        s = step * per_step + i
        columns = []
        for g in range(groups):
            blocks = []
            for c in range(GROUP):
                bucket = from_ref[g * GROUP + c]
                here = pl.multiple_of((bucket % CCAP * S + s) * HALF, HALF)
                blocks.append(in_ref[bucket // CCAP, pl.ds(here, HALF)])
            columns.append(jnp.concatenate(blocks, axis=0))
        moved = jnp.dot(perm, jnp.concatenate(columns, axis=1), preferred_element_type=jnp.float32)
        moved = moved.astype(jnp.bfloat16)
        for g in range(groups):
            mine = moved[:, g * LANES : (g + 1) * LANES]
            even, odd = mine[0:LANES], mine[LANES:]
            out_ref[i, g, 0:LANES] = jnp.where(low, even, swap_halves(odd))
            out_ref[i, g, LANES:] = jnp.where(low, swap_halves(even), odd)


def whole(shape):
    return pl.BlockSpec(shape, lambda *_: (0,) * len(shape))


def body(a_blocks, p_blocks, a_source, send_list, agg_local, coarse_slot, coarse_target):
    rows, per_row, _ = a_blocks.shape
    peers = lax.axis_size(("px", "py"))
    peers_y = lax.axis_size("py")
    slots = send_list.shape[2]
    coarse_here = rows // AGG
    groups = rows // GROUP
    pairs = (per_row + 3) // 4 * 2
    bf16 = jnp.bfloat16
    smem = pl.BlockSpec(memory_space=pltpu.SMEM)

    a_tiles = as_tiles(a_blocks.transpose(1, 0, 2))
    p_tiles = as_tiles(p_blocks)
    outgoing, own = pl.pallas_call(
        pack_kernel,
        in_specs=[smem, whole((groups, KROWS, LANES))],
        out_specs=[whole((peers * slots, HALF, LANES)), whole((rows, HALF, LANES))],
        out_shape=[
            jax.ShapeDtypeStruct((peers * slots, HALF, LANES), bf16),
            jax.ShapeDtypeStruct((rows, HALF, LANES), bf16),
        ],
        scratch_shapes=[pltpu.VMEM((rows + 1, HALF, LANES), bf16)],
        compiler_params=pltpu.CompilerParams(vmem_limit_bytes=24 * MIB),
    )(send_list[0].T, p_tiles)
    arrived = lax.all_to_all(
        outgoing.reshape(peers, slots, HALF, LANES), ("px", "py"), split_axis=0, concat_axis=0, tiled=True
    ).reshape(peers * slots, HALF, LANES)

    sums = coarse_here * S
    most_tiles = (rows * pairs + CHUNK - 1) // CHUNK * CHUNK
    local, tiles, meta, count = pl.pallas_call(
        functools.partial(project_kernel, peers * slots),
        grid=(groups,),
        in_specs=[
            smem, smem, smem,
            pl.BlockSpec((per_row, 1, KROWS, LANES), lambda g: (0, g, 0, 0)),
            pl.BlockSpec((1, KROWS, LANES), lambda g: (g, 0, 0)),
            whole((rows, HALF, LANES)),
        ],
        out_specs=[whole((sums, HALF, LANES)), pl.BlockSpec(memory_space=pl.ANY), smem, smem],
        out_shape=[
            jax.ShapeDtypeStruct((sums, HALF, LANES), jnp.float32),
            jax.ShapeDtypeStruct((most_tiles, B, LANES), bf16),
            jax.ShapeDtypeStruct((2, most_tiles + CHUNK), jnp.int32),
            jax.ShapeDtypeStruct((1,), jnp.int32),
        ],
        scratch_shapes=[
            pltpu.VMEM((GROUP * B, 2 * KROWS), bf16),
            pltpu.VMEM((rows + 1, B, LANES), bf16),
            pltpu.VMEM((rows + 1, B, LANES), bf16),
            pltpu.VMEM((sums, HALF, LANES), jnp.float32),
            pltpu.VMEM((GROUP * pairs + 1, B, LANES), bf16),
            pltpu.VMEM((GROUP * pairs + 1, B, LANES), bf16),
            pltpu.VMEM((most_tiles, B, LANES), bf16),
            pltpu.SMEM((1,), jnp.int32),
            pltpu.SemaphoreType.DMA((RING,)),
        ],
        compiler_params=pltpu.CompilerParams(vmem_limit_bytes=60 * MIB),
        cost_estimate=pl.CostEstimate(
            flops=4 * 512 * 512 * 128 * pairs * groups, bytes_accessed=45_000_000, transcendentals=0
        ),
    )(a_source.T, coarse_slot.T, agg_local, a_tiles, p_tiles, own)

    coarse_rows = CCAP * S * HALF + 16
    sent = pl.pallas_call(
        combine_kernel,
        in_specs=[
            smem, smem, smem,
            whole((peers * slots, HALF, LANES)),
            pl.BlockSpec(memory_space=pl.ANY),
            pl.BlockSpec(memory_space=pl.ANY),
        ],
        out_specs=whole((peers_y, coarse_rows, LANES)),
        out_shape=jax.ShapeDtypeStruct((peers_y, coarse_rows, LANES), bf16),
        scratch_shapes=[
            pltpu.VMEM((peers * slots + 1, B, LANES), bf16),
            pltpu.VMEM((sums + 1, HALF, LANES), jnp.float32),
            pltpu.VMEM((sums + 1, HALF, LANES), jnp.float32),
            pltpu.VMEM((RING, CHUNK, B, LANES), bf16),
            pltpu.SMEM((coarse_here,), jnp.int32),
            pltpu.SMEM((peers_y * CCAP,), jnp.int32),
            pltpu.SMEM((peers_y,), jnp.int32),
            pltpu.SemaphoreType.DMA,
            pltpu.SemaphoreType.DMA((RING,)),
        ],
        compiler_params=pltpu.CompilerParams(vmem_limit_bytes=56 * MIB),
    )(meta, count, coarse_target, arrived, local, tiles)

    received = lax.all_to_all(sent, "py", split_axis=0, concat_axis=0, tiled=True)

    per_step = 3
    out_groups = coarse_here // GROUP
    placed = pl.pallas_call(
        place_kernel,
        grid=(S // per_step,),
        in_specs=[whole((peers_y, coarse_rows, LANES))],
        out_specs=pl.BlockSpec((per_step, out_groups, KROWS, LANES), lambda s: (s, 0, 0, 0)),
        out_shape=jax.ShapeDtypeStruct((S, out_groups, KROWS, LANES), bf16),
        scratch_shapes=[pltpu.SMEM((coarse_here,), jnp.int32)],
        compiler_params=pltpu.CompilerParams(vmem_limit_bytes=24 * MIB),
    )(received)
    return from_tiles(placed).transpose(1, 0, 2)


def solution(mesh):
    rows = ("px", "py")
    in_specs = (
        P(rows, None, None),
        P(rows, None),
        P(rows, None),
        P(rows, None, None),
        P(rows),
        P(rows, None),
        P(rows),
    )
    return jax.shard_map(body, mesh=mesh, in_specs=in_specs, out_specs=P(rows, None, None), check_vma=False)
```

```python
import functools

import jax
import jax.numpy as jnp
from jax import lax
from jax.experimental import pallas as pl
from jax.experimental.pallas import tpu as pltpu
from jax.sharding import PartitionSpec as P

B = 64
FLAT = B * B
LANES = 128
HALF = B // 2
S = 27
AGG = 6
CCAP = 2
GROUP = 8
TILES = FLAT // LANES
KROWS = GROUP * TILES
PIECES = 3
PS = S // PIECES
CHUNK = 16
LIST = 128
STAGE = LIST + 2 * CHUNK
SPREAD = 1024
RING = 4
MIB = 1 << 20


def lane_low(rows):
    return lax.broadcasted_iota(jnp.int32, (rows, LANES), 1) < B


def swap_halves(x):
    return pltpu.roll(x, B, 1)


def as_tiles(x):
    lead, rows = x.shape[:-2], x.shape[-2]
    split = x.reshape(*lead, rows // GROUP, GROUP, TILES, LANES)
    return jnp.swapaxes(split, -3, -2).reshape(*lead, rows // GROUP, KROWS, LANES)


def from_tiles(x):
    lead, groups = x.shape[:-3], x.shape[-3]
    split = x.reshape(*lead, groups, TILES, GROUP, LANES)
    return jnp.swapaxes(split, -3, -2).reshape(*lead, groups * GROUP, FLAT)


def block_perm(transposed):
    block_axis, tile_axis = (1, 0) if transposed else (0, 1)
    shape = (KROWS, KROWS)
    block_row = lax.broadcasted_iota(jnp.int32, shape, block_axis)
    tile_row = lax.broadcasted_iota(jnp.int32, shape, tile_axis)
    same_r = (block_row // HALF) == (tile_row % GROUP)
    want = 2 * ((tile_row % LANES) // GROUP) + tile_row // LANES
    same_j = (block_row % HALF) == want
    return jnp.where(same_r & same_j, 1.0, 0.0).astype(jnp.bfloat16)


def pack_kernel(send_hbm, p_hbm, out_ref, own_hbm, send_ref, p_ref, table_ref, sems, send_sem, own_sem):
    groups = p_ref.shape[0]
    rows = groups * GROUP
    slots, peers = send_ref.shape
    get_send = pltpu.make_async_copy(send_hbm, send_ref, send_sem)
    get_send.start()

    def get(g):
        return pltpu.make_async_copy(p_hbm.at[pl.ds(g, 2)], p_ref.at[pl.ds(g, 2)], sems.at[g // 2])

    for g in range(0, groups, 2):
        get(g).start()
    perm = block_perm(False)
    low = lane_low(LANES)

    def to_blocks(g):
        top, bottom = p_ref[g, 0:LANES, :], p_ref[g, LANES:KROWS, :]
        even = jnp.where(low, top, swap_halves(bottom))
        odd = jnp.where(low, swap_halves(top), bottom)
        return jnp.concatenate([even, odd], axis=0)

    for g in range(0, groups, 2):
        get(g).wait()
        both = jnp.concatenate([to_blocks(g), to_blocks(g + 1)], axis=1)
        blocks = jnp.dot(perm, both, preferred_element_type=jnp.float32).astype(jnp.bfloat16)
        for h in range(2):
            piece = blocks[:, h * LANES : (h + 1) * LANES].reshape(GROUP, HALF, LANES)
            table_ref[pl.ds((g + h) * GROUP, GROUP)] = piece
    put_own = pltpu.make_async_copy(table_ref.at[pl.ds(0, rows)], own_hbm, own_sem)
    put_own.start()
    table_ref[rows] = jnp.zeros((HALF, LANES), jnp.bfloat16)
    get_send.wait()

    def fill(peer, carry):
        for slot in range(slots):
            wanted = send_ref[slot, peer]
            out_ref[peer * slots + slot] = table_ref[jnp.where(wanted < 0, rows, wanted)]
        return carry

    lax.fori_loop(0, peers, fill, 0, unroll=2)
    put_own.wait()


def fold(value, low):
    top, bottom = value[0:HALF], value[HALF:]
    return jnp.where(low, top, swap_halves(bottom)), jnp.where(low, swap_halves(top), bottom)


def project_kernel(
    ghosts, source_ref, slot_ref, agg_ref, a_ref, p_ref, own_ref, sum_ref, tiles_hbm, meta_ref, count_ref,
    left_ref, first_ref, second_ref, odd_ref, even_tiles, odd_tiles, stage_ref,
    words_vec, words_ref, here_ref, done_ref, flying_ref, words_sem, sems,
):
    step = pl.program_id(0)
    last = pl.num_programs(0) - 1
    per_row, rows = source_ref.shape
    pairs = (per_row + 3) // 4 * 2
    sums = sum_ref.shape[0] // PIECES
    low_half, low_all = lane_low(HALF), lane_low(B)
    zero_all = jnp.zeros((B, LANES), jnp.bfloat16)

    @pl.when(step == 0)
    def _():
        source, slot = source_ref[...], slot_ref[...]
        part = (slot >= PS).astype(jnp.int32)
        for i in range(2, PIECES):
            part += (slot >= i * PS).astype(jnp.int32)
        place = agg_ref[...] * PS + slot - part * PS
        ghost = (source >= rows).astype(jnp.int32)
        words_vec[0] = (part * sums + place) * LIST + jnp.minimum(source, rows)
        words_vec[1] = jnp.maximum(source - rows, 0) * SPREAD + place
        words_vec[2] = part * 8 + ghost * 32
        load = pltpu.make_async_copy(words_vec, words_ref, words_sem)
        load.start()
        for i in range(PIECES):
            done_ref[i] = 0
            flying_ref[i] = 0

        def expand(i, carry):
            block = own_ref[i]
            turned = swap_halves(block)
            zero = jnp.zeros((HALF, LANES), jnp.bfloat16)
            first_ref[i, 0:HALF] = jnp.where(low_half, block, zero)
            first_ref[i, HALF:] = jnp.where(low_half, turned, zero)
            second_ref[i, 0:HALF] = jnp.where(low_half, zero, turned)
            second_ref[i, HALF:] = jnp.where(low_half, zero, block)
            return carry

        lax.fori_loop(0, rows, expand, 0, unroll=8)
        first_ref[rows] = zero_all
        second_ref[rows] = zero_all

        def clear(i, carry):
            for part in range(PIECES):
                sum_ref[part * sums + i] = jnp.zeros((HALF, LANES), jnp.float32)
                odd_ref[part * sums + i] = jnp.zeros((HALF, LANES), jnp.float32)
            return carry

        lax.fori_loop(0, sums, clear, 0, unroll=4)
        load.wait()

    flipped = p_ref[0].T
    row_of = lax.broadcasted_iota(jnp.int32, (B, KROWS), 1) % GROUP
    zero = jnp.zeros((B, KROWS), jnp.bfloat16)
    for r in range(GROUP):
        mine = row_of == r
        left_ref[r * B : (r + 1) * B, 0:KROWS] = jnp.where(mine, flipped[0:B], zero)
        left_ref[r * B : (r + 1) * B, KROWS:] = jnp.where(mine, flipped[B:], zero)
    low = lane_low(KROWS)

    def pair_of(pair):
        first = a_ref[2 * pair, 0]
        second = a_ref[min(2 * pair + 1, per_row - 1), 0]
        even = jnp.where(low, first, swap_halves(second))
        odd = jnp.where(low, swap_halves(first), second)
        return jnp.concatenate([even, odd], axis=0)

    counts = [jnp.int32(0), jnp.int32(0)]
    for pair in range(0, pairs, 2):
        right = jnp.concatenate([pair_of(pair), pair_of(pair + 1)], axis=1)
        both = jnp.dot(left_ref[...], right, preferred_element_type=jnp.float32).astype(jnp.bfloat16)
        for r in range(GROUP):
            row = step * GROUP + r
            moving = both[r * B : (r + 1) * B]
            weights, targets = [], []
            for h in range(2):
                tile = moving[:, h * LANES : (h + 1) * LANES]
                halves = []
                for parity, table, listed in ((0, first_ref, even_tiles), (1, second_ref, odd_tiles)):
                    k = 2 * (pair + h) + parity
                    if k >= per_row:
                        halves.append(zero_all)
                        targets.append(None)
                        continue
                    word = words_ref[0, k, row]
                    halves.append(table[word % LIST])
                    targets.append(word // LIST)
                    if k > 0:
                        flags = words_ref[2, k, row]
                        shift = flags % 32
                        at = (counts[parity] >> shift) % LIST + shift * (LIST // 8)
                        listed[at] = tile
                        here_ref[parity, at] = words_ref[1, k, row]
                        counts[parity] += (flags // 32) << shift
                filled = jnp.concatenate(halves, axis=0)
                blank = jnp.zeros_like(filled)
                weights.append(jnp.concatenate([filled, blank] if h == 0 else [blank, filled], axis=1))
            value = jnp.dot(moving, jnp.concatenate(weights, axis=0), preferred_element_type=jnp.float32)
            for h in range(2):
                even, odd = fold(value[:, h * LANES : (h + 1) * LANES], low_half)
                sum_ref[targets[2 * h]] += even
                if targets[2 * h + 1] is not None:
                    odd_ref[targets[2 * h + 1]] += odd

    no_entry = ghosts * SPREAD + sums
    for part in range(PIECES):
        even_count = (counts[0] >> (8 * part)) % LIST
        odd_count = (counts[1] >> (8 * part)) % LIST
        after = jnp.maximum(even_count, odd_count)
        before = done_ref[part]
        chunks = (after + CHUNK - 1) // CHUNK + jnp.where(step == last, 1, 0)

        def copy(i, start, part=part):
            return pltpu.make_async_copy(
                stage_ref.at[part, pl.ds(i * CHUNK, CHUNK)],
                tiles_hbm.at[part, pl.ds(start + i * CHUNK, CHUNK)],
                sems.at[part, i],
            )

        def finish(i, carry, copy=copy):
            copy(i, 0).wait()
            return carry

        lax.fori_loop(0, flying_ref[part], finish, 0)

        def merge(i, carry, part=part, even_count=even_count, odd_count=odd_count, before=before):
            end = part * LIST + jnp.minimum(i, LIST - 1)
            keep_even, keep_odd = i < even_count, i < odd_count
            even_at = jnp.where(low_all, i, LIST + CHUNK * 2) < even_count
            odd_at = jnp.where(low_all, LIST + CHUNK * 2, i) < odd_count
            tile = jnp.where(even_at, even_tiles[end], zero_all)
            stage_ref[part, i] = jnp.where(odd_at, odd_tiles[end], tile)
            meta_ref[2 * part, before + i] = jnp.where(keep_even, here_ref[0, end], no_entry)
            meta_ref[2 * part + 1, before + i] = jnp.where(keep_odd, here_ref[1, end], no_entry)
            return carry

        lax.fori_loop(0, jnp.where(step == last, chunks * CHUNK, after), merge, 0)

        def send(i, carry, copy=copy, before=before):
            copy(i, before).start()
            return carry

        lax.fori_loop(0, chunks, send, 0)
        flying_ref[part] = chunks
        done_ref[part] = before + after

    @pl.when(step == last)
    def _():
        def total(i, carry):
            for part in range(PIECES):
                sum_ref[part * sums + i] += odd_ref[part * sums + i]
            return carry

        lax.fori_loop(0, sums, total, 0, unroll=4)
        for part in range(PIECES):
            count_ref[part] = (done_ref[part] + CHUNK - 1) // CHUNK

            def drain(i, carry, part=part):
                pltpu.make_async_copy(
                    stage_ref.at[part, pl.ds(i * CHUNK, CHUNK)],
                    tiles_hbm.at[part, pl.ds(i * CHUNK, CHUNK)],
                    sems.at[part, i],
                ).wait()
                return carry

            lax.fori_loop(0, flying_ref[part], drain, 0)


def combine_kernel(
    part, meta_ref, count_ref, target_ref, ghost_ref, sum_hbm, tiles_hbm, out_ref,
    table_ref, even_ref, odd_ref, tiles_ref, bucket_ref, place_ref, per_peer_ref, sum_sem, sems,
):
    ghosts = ghost_ref.shape[0]
    coarse_here = target_ref.shape[0]
    sums = coarse_here * PS
    peers = out_ref.shape[0]
    chunks = count_ref[part]
    low_half, low_all = lane_low(HALF), lane_low(B)
    zero_all = jnp.zeros((B, LANES), jnp.bfloat16)
    load_sums = pltpu.make_async_copy(sum_hbm.at[pl.ds(part * sums, sums)], even_ref.at[pl.ds(0, sums)], sum_sem)
    load_sums.start()

    def fetch(i):
        slot = i % RING
        return pltpu.make_async_copy(tiles_hbm.at[part, pl.ds(i * CHUNK, CHUNK)], tiles_ref.at[slot], sems.at[slot])

    for i in range(RING - 1):

        @pl.when(i < chunks)
        def _():
            fetch(i).start()

    def expand(i, carry):
        block = ghost_ref[i]
        turned = swap_halves(block)
        table_ref[i, 0:HALF] = jnp.where(low_half, block, turned)
        table_ref[i, HALF:] = jnp.where(low_half, turned, block)
        return carry

    lax.fori_loop(0, ghosts, expand, 0, unroll=8)
    table_ref[ghosts] = zero_all

    def clear(i, carry):
        odd_ref[i] = jnp.zeros((HALF, LANES), jnp.float32)
        return carry

    lax.fori_loop(0, sums, clear, 0, unroll=8)

    for p in range(peers):
        per_peer_ref[p] = 0
        for q in range(CCAP):
            place_ref[p * CCAP + q] = -1

    def assign(c, carry):
        target = target_ref[c]
        peer = target // coarse_here % peers
        bucket = peer * CCAP + per_peer_ref[peer]
        per_peer_ref[peer] = per_peer_ref[peer] + 1
        bucket_ref[c] = bucket
        place_ref[bucket] = target % coarse_here
        return carry

    lax.fori_loop(0, coarse_here, assign, 0)
    payload = CCAP * PS * HALF
    second_slot = lax.broadcasted_iota(jnp.int32, (out_ref.shape[1] - payload, LANES), 1) // HALF % CCAP

    def note(p, carry):
        value = jnp.full(second_slot.shape, -1, jnp.int32)
        for q in range(CCAP):
            value = jnp.where(second_slot == q, place_ref[p * CCAP + q], value)
        out_ref[p, payload:] = value.astype(jnp.float32).astype(jnp.bfloat16)
        return carry

    lax.fori_loop(0, peers, note, 0)
    load_sums.wait()

    def work(i, carry):
        @pl.when(i + RING - 1 < chunks)
        def _():
            fetch(i + RING - 1).start()

        fetch(i).wait()
        slot = i % RING
        for j in range(0, CHUNK, 2):
            weights, targets = [], []
            for h in range(2):
                at = i * CHUNK + j + h
                even, odd = meta_ref[2 * part, at], meta_ref[2 * part + 1, at]
                upper = jnp.where(low_all, table_ref[even // SPREAD], zero_all)
                lower = jnp.where(low_all, zero_all, table_ref[odd // SPREAD])
                targets += [even % SPREAD, odd % SPREAD]
                filled = jnp.concatenate([upper, lower], axis=0)
                blank = jnp.zeros_like(filled)
                weights.append(jnp.concatenate([filled, blank] if h == 0 else [blank, filled], axis=1))
            moving = jnp.concatenate([tiles_ref[slot, j], tiles_ref[slot, j + 1]], axis=1)
            value = jnp.dot(moving, jnp.concatenate(weights, axis=0), preferred_element_type=jnp.float32)
            for h in range(2):
                even, odd = fold(value[:, h * LANES : (h + 1) * LANES], low_half)
                even_ref[targets[2 * h]] += even
                odd_ref[targets[2 * h + 1]] += odd
        return carry

    lax.fori_loop(0, chunks, work, 0)

    def finish(c, carry):
        bucket = bucket_ref[c]
        start = bucket % CCAP * (PS * HALF)
        for s in range(PS):
            total = even_ref[c * PS + s] + odd_ref[c * PS + s]
            here = pl.multiple_of(start + s * HALF, HALF)
            out_ref[bucket // CCAP, pl.ds(here, HALF)] = total.astype(jnp.bfloat16)
        return carry

    lax.fori_loop(0, coarse_here, finish, 0)


def place_kernel(in_ref, *rest):
    out_ref, from_ref = rest[-2:]
    step = pl.program_id(0)
    peers = in_ref.shape[0]
    per_step, groups = out_ref.shape[0], out_ref.shape[1]
    payload = CCAP * PS * HALF

    @pl.when(step == 0)
    def _():
        for p in range(peers):
            notes = in_ref[p, payload:].astype(jnp.float32)
            which = lax.broadcasted_iota(jnp.int32, notes.shape, 1) // HALF
            for q in range(CCAP):
                place = jnp.max(jnp.where(which == q, notes, -1.0)).astype(jnp.int32)

                @pl.when(place >= 0)
                def _():
                    from_ref[place] = p * CCAP + q

    perm = block_perm(True)
    low = lane_low(LANES)
    for i in range(per_step):
        s = step * per_step + i
        columns = []
        for g in range(groups):
            blocks = []
            for c in range(GROUP):
                bucket = from_ref[g * GROUP + c]
                here = pl.multiple_of((bucket % CCAP * PS + s) * HALF, HALF)
                blocks.append(in_ref[bucket // CCAP, pl.ds(here, HALF)])
            columns.append(jnp.concatenate(blocks, axis=0))
        moved = jnp.dot(perm, jnp.concatenate(columns, axis=1), preferred_element_type=jnp.float32)
        moved = moved.astype(jnp.bfloat16)
        for g in range(groups):
            mine = moved[:, g * LANES : (g + 1) * LANES]
            even, odd = mine[0:LANES], mine[LANES:]
            out_ref[i, g, 0:LANES] = jnp.where(low, even, swap_halves(odd))
            out_ref[i, g, LANES:] = jnp.where(low, swap_halves(even), odd)


def whole(shape):
    return pl.BlockSpec(shape, lambda *_: (0,) * len(shape))


def body(a_blocks, p_blocks, a_source, send_list, agg_local, coarse_slot, coarse_target):
    rows, per_row, _ = a_blocks.shape
    peers = lax.axis_size(("px", "py"))
    peers_y = lax.axis_size("py")
    slots = send_list.shape[2]
    coarse_here = rows // AGG
    groups = rows // GROUP
    pairs = (per_row + 3) // 4 * 2
    bf16 = jnp.bfloat16
    smem = pl.BlockSpec(memory_space=pltpu.SMEM)

    a_tiles = as_tiles(a_blocks.transpose(1, 0, 2))
    p_tiles = as_tiles(p_blocks)
    hbm = pl.BlockSpec(memory_space=pltpu.HBM)
    outgoing, own = pl.pallas_call(
        pack_kernel,
        in_specs=[hbm, hbm],
        out_specs=[whole((peers * slots, HALF, LANES)), hbm],
        out_shape=[
            jax.ShapeDtypeStruct((peers * slots, HALF, LANES), bf16),
            jax.ShapeDtypeStruct((rows, HALF, LANES), bf16),
        ],
        scratch_shapes=[
            pltpu.SMEM((slots, peers), jnp.int32),
            pltpu.VMEM((groups, KROWS, LANES), bf16),
            pltpu.VMEM((rows + 1, HALF, LANES), bf16),
            pltpu.SemaphoreType.DMA((groups // 2,)),
            pltpu.SemaphoreType.DMA,
            pltpu.SemaphoreType.DMA,
        ],
        compiler_params=pltpu.CompilerParams(vmem_limit_bytes=24 * MIB),
    )(send_list[0].T, p_tiles)
    arrived = lax.all_to_all(
        outgoing.reshape(peers, slots, HALF, LANES), ("px", "py"), split_axis=0, concat_axis=0, tiled=True
    ).reshape(peers * slots, HALF, LANES)

    sums = coarse_here * PS
    room = groups * LIST + STAGE
    local, tiles, meta, count = pl.pallas_call(
        functools.partial(project_kernel, peers * slots),
        grid=(groups,),
        in_specs=[
            whole((per_row, rows)),
            whole((per_row, rows)),
            whole((1, rows)),
            pl.BlockSpec((per_row, 1, KROWS, LANES), lambda g: (0, g, 0, 0)),
            pl.BlockSpec((1, KROWS, LANES), lambda g: (g, 0, 0)),
            whole((rows, HALF, LANES)),
        ],
        out_specs=[whole((PIECES * sums, HALF, LANES)), hbm, smem, smem],
        out_shape=[
            jax.ShapeDtypeStruct((PIECES * sums, HALF, LANES), jnp.float32),
            jax.ShapeDtypeStruct((PIECES, room, B, LANES), bf16),
            jax.ShapeDtypeStruct((2 * PIECES, room), jnp.int32),
            jax.ShapeDtypeStruct((PIECES,), jnp.int32),
        ],
        scratch_shapes=[
            pltpu.VMEM((GROUP * B, 2 * KROWS), bf16),
            pltpu.VMEM((rows + 1, B, LANES), bf16),
            pltpu.VMEM((rows + 1, B, LANES), bf16),
            pltpu.VMEM((PIECES * sums, HALF, LANES), jnp.float32),
            pltpu.VMEM((PIECES * LIST, B, LANES), bf16),
            pltpu.VMEM((PIECES * LIST, B, LANES), bf16),
            pltpu.VMEM((PIECES, STAGE, B, LANES), bf16),
            pltpu.VMEM((3, per_row, rows), jnp.int32),
            pltpu.SMEM((3, per_row, rows), jnp.int32),
            pltpu.SMEM((2, PIECES * LIST), jnp.int32),
            pltpu.SMEM((PIECES,), jnp.int32),
            pltpu.SMEM((PIECES,), jnp.int32),
            pltpu.SemaphoreType.DMA,
            pltpu.SemaphoreType.DMA((PIECES, STAGE // CHUNK)),
        ],
        compiler_params=pltpu.CompilerParams(vmem_limit_bytes=58 * MIB),
        cost_estimate=pl.CostEstimate(
            flops=4 * 512 * 512 * 128 * pairs * groups, bytes_accessed=45_000_000, transcendentals=0
        ),
    )(a_source.T, coarse_slot.T, agg_local.reshape(1, rows), a_tiles, p_tiles, own)

    piece_rows = CCAP * PS * HALF + 16
    received = []
    for part in range(PIECES):
        sent = pl.pallas_call(
            functools.partial(combine_kernel, part),
            in_specs=[smem, smem, smem, whole((peers * slots, HALF, LANES)), hbm, hbm],
            out_specs=whole((peers_y, piece_rows, LANES)),
            out_shape=jax.ShapeDtypeStruct((peers_y, piece_rows, LANES), bf16),
            scratch_shapes=[
                pltpu.VMEM((peers * slots + 1, B, LANES), bf16),
                pltpu.VMEM((sums + 1, HALF, LANES), jnp.float32),
                pltpu.VMEM((sums + 1, HALF, LANES), jnp.float32),
                pltpu.VMEM((RING, CHUNK, B, LANES), bf16),
                pltpu.SMEM((coarse_here,), jnp.int32),
                pltpu.SMEM((peers_y * CCAP,), jnp.int32),
                pltpu.SMEM((peers_y,), jnp.int32),
                pltpu.SemaphoreType.DMA,
                pltpu.SemaphoreType.DMA((RING,)),
            ],
            compiler_params=pltpu.CompilerParams(vmem_limit_bytes=16 * MIB + peers * slots * 28 * 1024),
            cost_estimate=pl.CostEstimate(flops=4_000_000_000, bytes_accessed=8_000_000, transcendentals=0),
        )(meta, count, coarse_target, arrived, local, tiles)
        received.append(lax.all_to_all(sent, "py", split_axis=0, concat_axis=0, tiled=True))

    per_step = 3
    out_groups = coarse_here // GROUP
    placed = None
    for part in range(PIECES):
        first = part * PS // per_step
        placed = pl.pallas_call(
            place_kernel,
            grid=(PS // per_step,),
            in_specs=[whole((peers_y, piece_rows, LANES))] + ([hbm] if part else []),
            out_specs=pl.BlockSpec((per_step, out_groups, KROWS, LANES), lambda s, first=first: (first + s, 0, 0, 0)),
            out_shape=jax.ShapeDtypeStruct((S, out_groups, KROWS, LANES), bf16),
            scratch_shapes=[pltpu.SMEM((coarse_here,), jnp.int32)],
            input_output_aliases={1: 0} if part else {},
            compiler_params=pltpu.CompilerParams(vmem_limit_bytes=24 * MIB),
            cost_estimate=pl.CostEstimate(flops=1_000_000_000, bytes_accessed=3_000_000, transcendentals=0),
        )(received[part], *([placed] if part else []))
    return from_tiles(placed).transpose(1, 0, 2)


def solution(mesh):
    rows = ("px", "py")
    in_specs = (
        P(rows, None, None),
        P(rows, None),
        P(rows, None),
        P(rows, None, None),
        P(rows),
        P(rows, None),
        P(rows),
    )
    return jax.shard_map(body, mesh=mesh, in_specs=in_specs, out_specs=P(rows, None, None), check_vma=False)
```

```python
import functools

import jax
import jax.numpy as jnp
from jax import lax
from jax.experimental import pallas as pl
from jax.experimental.pallas import tpu as pltpu
from jax.sharding import PartitionSpec as P

B = 64
FLAT = B * B
LANES = 128
HALF = B // 2
S = 27
AGG = 6
CCAP = 2
GROUP = 8
TILES = FLAT // LANES
KROWS = GROUP * TILES
PIECES = 1
PS = S // PIECES
CHUNK = 32
TURN = 8
LIST = 128
STAGE = LIST + 2 * CHUNK
SRC_BITS = 7
PLACE_BITS = 10
FLAG_BIT = 30
RING = 4
MIB = 1 << 20


def lane_low(rows):
    return lax.broadcasted_iota(jnp.int32, (rows, LANES), 1) < B


def swap_halves(x):
    return pltpu.roll(x, B, 1)


def as_tiles(x):
    lead, rows = x.shape[:-2], x.shape[-2]
    split = x.reshape(*lead, rows // GROUP, GROUP, TILES, LANES)
    return jnp.swapaxes(split, -3, -2).reshape(*lead, rows // GROUP, KROWS, LANES)


def from_tiles(x):
    lead, groups = x.shape[:-3], x.shape[-3]
    split = x.reshape(*lead, groups, TILES, GROUP, LANES)
    return jnp.swapaxes(split, -3, -2).reshape(*lead, groups * GROUP, FLAT)


def block_perm(transposed):
    block_axis, tile_axis = (1, 0) if transposed else (0, 1)
    shape = (KROWS, KROWS)
    block_row = lax.broadcasted_iota(jnp.int32, shape, block_axis)
    tile_row = lax.broadcasted_iota(jnp.int32, shape, tile_axis)
    same_r = (block_row // HALF) == (tile_row % GROUP)
    want = 2 * ((tile_row % LANES) // GROUP) + tile_row // LANES
    same_j = (block_row % HALF) == want
    return jnp.where(same_r & same_j, 1.0, 0.0).astype(jnp.bfloat16)


def pack_kernel(send_hbm, p_hbm, out_ref, own_hbm, send_ref, p_ref, table_ref, sems, send_sem, own_sem):
    groups = p_ref.shape[0]
    rows = groups * GROUP
    slots, peers = send_ref.shape
    get_send = pltpu.make_async_copy(send_hbm, send_ref, send_sem)
    get_send.start()

    def get(g):
        return pltpu.make_async_copy(p_hbm.at[pl.ds(g, 2)], p_ref.at[pl.ds(g, 2)], sems.at[g // 2])

    for g in range(0, groups, 2):
        get(g).start()
    perm = block_perm(False)
    low = lane_low(LANES)

    def to_blocks(g):
        top, bottom = p_ref[g, 0:LANES, :], p_ref[g, LANES:KROWS, :]
        even = jnp.where(low, top, swap_halves(bottom))
        odd = jnp.where(low, swap_halves(top), bottom)
        return jnp.concatenate([even, odd], axis=0)

    for g in range(0, groups, 2):
        get(g).wait()
        both = jnp.concatenate([to_blocks(g), to_blocks(g + 1)], axis=1)
        blocks = jnp.dot(perm, both, preferred_element_type=jnp.float32).astype(jnp.bfloat16)
        for h in range(2):
            piece = blocks[:, h * LANES : (h + 1) * LANES].reshape(GROUP, HALF, LANES)
            table_ref[pl.ds((g + h) * GROUP, GROUP)] = piece
    put_own = pltpu.make_async_copy(table_ref.at[pl.ds(0, rows)], own_hbm, own_sem)
    put_own.start()
    table_ref[rows] = jnp.zeros((HALF, LANES), jnp.bfloat16)
    get_send.wait()

    def fill(peer, carry):
        for slot in range(slots):
            wanted = send_ref[slot, peer]
            out_ref[peer * slots + slot] = table_ref[jnp.where(wanted < 0, rows, wanted)]
        return carry

    lax.fori_loop(0, peers, fill, 0, unroll=2)
    put_own.wait()


def fold(value, low):
    top, bottom = value[0:HALF], value[HALF:]
    return jnp.where(low, top, swap_halves(bottom)), jnp.where(low, swap_halves(top), bottom)


def project_kernel(
    ghosts, source_ref, slot_ref, agg_ref, a_ref, p_ref, own_ref, sum_ref, tiles_hbm, meta_ref, count_ref,
    left_ref, first_ref, second_ref, odd_ref, even_tiles, odd_tiles, stage_ref,
    words_vec, words_ref, here_ref, done_ref, flying_ref, words_sem, sems,
):
    step = pl.program_id(0)
    last = pl.num_programs(0) - 1
    per_row, rows = source_ref.shape
    pairs = (per_row + 3) // 4 * 2
    sums = sum_ref.shape[0] // PIECES
    low_half, low_all = lane_low(HALF), lane_low(B)
    zero_all = jnp.zeros((B, LANES), jnp.bfloat16)

    @pl.when(step == 0)
    def _():
        source, slot = source_ref[...], slot_ref[...]
        part = (slot >= PS).astype(jnp.int32)
        for i in range(2, PIECES):
            part += (slot >= i * PS).astype(jnp.int32)
        place = agg_ref[...] * PS + slot - part * PS
        ghost = (source >= rows).astype(jnp.int32)
        words_vec[0] = ((part * sums + place) << SRC_BITS) + jnp.minimum(source, rows)
        words_vec[1] = (ghost << FLAG_BIT) + (jnp.maximum(source - rows, 0) << PLACE_BITS) + place
        load = pltpu.make_async_copy(words_vec, words_ref, words_sem)
        load.start()
        for i in range(PIECES):
            done_ref[i] = 0
            flying_ref[i] = 0

        def expand(i, carry):
            block = own_ref[i]
            turned = swap_halves(block)
            zero = jnp.zeros((HALF, LANES), jnp.bfloat16)
            first_ref[i, 0:HALF] = jnp.where(low_half, block, zero)
            first_ref[i, HALF:] = jnp.where(low_half, turned, zero)
            second_ref[i, 0:HALF] = jnp.where(low_half, zero, turned)
            second_ref[i, HALF:] = jnp.where(low_half, zero, block)
            return carry

        lax.fori_loop(0, rows, expand, 0, unroll=8)
        first_ref[rows] = zero_all
        second_ref[rows] = zero_all

        def clear(i, carry):
            for part in range(PIECES):
                sum_ref[part * sums + i] = jnp.zeros((HALF, LANES), jnp.float32)
                odd_ref[part * sums + i] = jnp.zeros((HALF, LANES), jnp.float32)
            return carry

        lax.fori_loop(0, sums, clear, 0, unroll=4)
        load.wait()

    flipped = p_ref[0].T
    row_of = lax.broadcasted_iota(jnp.int32, (B, KROWS), 1) % GROUP
    zero = jnp.zeros((B, KROWS), jnp.bfloat16)
    for r in range(GROUP):
        mine = row_of == r
        left_ref[r * B : (r + 1) * B, 0:KROWS] = jnp.where(mine, flipped[0:B], zero)
        left_ref[r * B : (r + 1) * B, KROWS:] = jnp.where(mine, flipped[B:], zero)
    low = lane_low(KROWS)

    def pair_of(pair):
        first = a_ref[2 * pair, 0]
        second = a_ref[min(2 * pair + 1, per_row - 1), 0]
        even = jnp.where(low, first, swap_halves(second))
        odd = jnp.where(low, swap_halves(first), second)
        return jnp.concatenate([even, odd], axis=0)

    counts = [jnp.int32(0), jnp.int32(0)]
    for pair in range(0, pairs, 2):
        right = jnp.concatenate([pair_of(pair), pair_of(pair + 1)], axis=1)
        both = jnp.dot(left_ref[...], right, preferred_element_type=jnp.float32).astype(jnp.bfloat16)
        for r in range(GROUP):
            row = step * GROUP + r
            moving = both[r * B : (r + 1) * B]
            weights, targets = [], []
            for h in range(2):
                tile = moving[:, h * LANES : (h + 1) * LANES]
                halves = []
                for parity, table, listed in ((0, first_ref, even_tiles), (1, second_ref, odd_tiles)):
                    k = 2 * (pair + h) + parity
                    if k >= per_row:
                        halves.append(zero_all)
                        targets.append(None)
                        continue
                    word = words_ref[0, k, row]
                    halves.append(table[word & ((1 << SRC_BITS) - 1)])
                    targets.append(word >> SRC_BITS)
                    if k > 0:
                        at = counts[parity]
                        note = words_ref[1, k, row]
                        listed[at] = tile
                        here_ref[parity, at] = note
                        counts[parity] = at + (note >> FLAG_BIT)
                filled = jnp.concatenate(halves, axis=0)
                blank = jnp.zeros_like(filled)
                weights.append(jnp.concatenate([filled, blank] if h == 0 else [blank, filled], axis=1))
            value = jnp.dot(moving, jnp.concatenate(weights, axis=0), preferred_element_type=jnp.float32)
            for h in range(2):
                even, odd = fold(value[:, h * LANES : (h + 1) * LANES], low_half)
                sum_ref[targets[2 * h]] += even
                if targets[2 * h + 1] is not None:
                    odd_ref[targets[2 * h + 1]] += odd

    no_entry = (ghosts << PLACE_BITS) + sums
    for part in range(PIECES):
        even_count, odd_count = counts
        after = jnp.maximum(even_count, odd_count)
        before = done_ref[part]
        chunks = lax.div(after + CHUNK - 1, CHUNK) + jnp.where(step == last, 1, 0)

        def copy(i, start, part=part):
            return pltpu.make_async_copy(
                stage_ref.at[part, pl.ds(i * CHUNK, CHUNK)],
                tiles_hbm.at[part, pl.ds(start + i * CHUNK, CHUNK)],
                sems.at[part, i],
            )

        def finish(i, carry, copy=copy):
            copy(i, 0).wait()
            return carry

        lax.fori_loop(0, flying_ref[part], finish, 0)

        def merge(turn, carry, part=part, even_count=even_count, odd_count=odd_count, before=before):
            for j in range(TURN):
                i = turn * TURN + j
                end = part * LIST + jnp.minimum(i, LIST - 1)
                even_at = jnp.where(low_all, i, STAGE) < even_count
                odd_at = jnp.where(low_all, STAGE, i) < odd_count
                tile = jnp.where(even_at, even_tiles[end], zero_all)
                stage_ref[part, i] = jnp.where(odd_at, odd_tiles[end], tile)
                meta_ref[2 * part, before + i] = jnp.where(i < even_count, here_ref[0, end], no_entry)
                meta_ref[2 * part + 1, before + i] = jnp.where(i < odd_count, here_ref[1, end], no_entry)
            return carry

        turns = jnp.where(step == last, chunks * (CHUNK // TURN), (after + TURN - 1) >> 3)
        lax.fori_loop(0, turns, merge, 0)

        def send(i, carry, copy=copy, before=before):
            copy(i, before).start()
            return carry

        lax.fori_loop(0, chunks, send, 0)
        flying_ref[part] = chunks
        done_ref[part] = before + after

    @pl.when(step == last)
    def _():
        def total(i, carry):
            for part in range(PIECES):
                sum_ref[part * sums + i] += odd_ref[part * sums + i]
            return carry

        lax.fori_loop(0, sums, total, 0, unroll=4)
        for part in range(PIECES):
            count_ref[part] = lax.div(done_ref[part] + CHUNK - 1, CHUNK)

            def drain(i, carry, part=part):
                pltpu.make_async_copy(
                    stage_ref.at[part, pl.ds(i * CHUNK, CHUNK)],
                    tiles_hbm.at[part, pl.ds(i * CHUNK, CHUNK)],
                    sems.at[part, i],
                ).wait()
                return carry

            lax.fori_loop(0, flying_ref[part], drain, 0)


def combine_kernel(
    part, meta_ref, count_ref, target_ref, ghost_ref, sum_hbm, tiles_hbm, out_ref,
    table_ref, even_ref, odd_ref, tiles_ref, bucket_ref, place_ref, per_peer_ref, sum_sem, sems,
):
    ghosts = ghost_ref.shape[0]
    coarse_here = target_ref.shape[0]
    sums = coarse_here * PS
    peers = out_ref.shape[0]
    chunks = count_ref[part]
    low_half, low_all = lane_low(HALF), lane_low(B)
    zero_all = jnp.zeros((B, LANES), jnp.bfloat16)
    load_sums = pltpu.make_async_copy(sum_hbm.at[pl.ds(part * sums, sums)], even_ref.at[pl.ds(0, sums)], sum_sem)
    load_sums.start()

    def fetch(i):
        slot = lax.rem(i, RING)
        return pltpu.make_async_copy(tiles_hbm.at[part, pl.ds(i * CHUNK, CHUNK)], tiles_ref.at[slot], sems.at[slot])

    for i in range(RING - 1):

        @pl.when(i < chunks)
        def _():
            fetch(i).start()

    def expand(i, carry):
        block = ghost_ref[i]
        turned = swap_halves(block)
        table_ref[i, 0:HALF] = jnp.where(low_half, block, turned)
        table_ref[i, HALF:] = jnp.where(low_half, turned, block)
        return carry

    lax.fori_loop(0, ghosts, expand, 0, unroll=8)
    table_ref[ghosts] = zero_all

    def clear(i, carry):
        odd_ref[i] = jnp.zeros((HALF, LANES), jnp.float32)
        return carry

    lax.fori_loop(0, sums, clear, 0, unroll=8)

    for p in range(peers):
        per_peer_ref[p] = 0
        for q in range(CCAP):
            place_ref[p * CCAP + q] = -1

    def assign(c, carry):
        target = target_ref[c]
        peer = lax.rem(lax.div(target, coarse_here), peers)
        bucket = peer * CCAP + per_peer_ref[peer]
        per_peer_ref[peer] = per_peer_ref[peer] + 1
        bucket_ref[c] = bucket
        place_ref[bucket] = lax.rem(target, coarse_here)
        return carry

    lax.fori_loop(0, coarse_here, assign, 0)
    payload = CCAP * PS * HALF
    second_slot = lax.broadcasted_iota(jnp.int32, (out_ref.shape[1] - payload, LANES), 1) // HALF % CCAP

    def note(p, carry):
        value = jnp.full(second_slot.shape, -1, jnp.int32)
        for q in range(CCAP):
            value = jnp.where(second_slot == q, place_ref[p * CCAP + q], value)
        out_ref[p, payload:] = value.astype(jnp.float32).astype(jnp.bfloat16)
        return carry

    lax.fori_loop(0, peers, note, 0)
    load_sums.wait()

    def work(i, carry):
        @pl.when(i + RING - 1 < chunks)
        def _():
            fetch(i + RING - 1).start()

        fetch(i).wait()
        slot = lax.rem(i, RING)
        for j in range(0, CHUNK, 2):
            weights, targets = [], []
            for h in range(2):
                at = i * CHUNK + j + h
                even, odd = meta_ref[2 * part, at], meta_ref[2 * part + 1, at]
                upper = jnp.where(low_all, table_ref[(even >> PLACE_BITS) & ((1 << FLAG_BIT - PLACE_BITS) - 1)], zero_all)
                lower = jnp.where(low_all, zero_all, table_ref[(odd >> PLACE_BITS) & ((1 << FLAG_BIT - PLACE_BITS) - 1)])
                targets += [even & ((1 << PLACE_BITS) - 1), odd & ((1 << PLACE_BITS) - 1)]
                filled = jnp.concatenate([upper, lower], axis=0)
                blank = jnp.zeros_like(filled)
                weights.append(jnp.concatenate([filled, blank] if h == 0 else [blank, filled], axis=1))
            moving = jnp.concatenate([tiles_ref[slot, j], tiles_ref[slot, j + 1]], axis=1)
            value = jnp.dot(moving, jnp.concatenate(weights, axis=0), preferred_element_type=jnp.float32)
            for h in range(2):
                even, odd = fold(value[:, h * LANES : (h + 1) * LANES], low_half)
                even_ref[targets[2 * h]] += even
                odd_ref[targets[2 * h + 1]] += odd
        return carry

    lax.fori_loop(0, chunks, work, 0)

    def finish(c, carry):
        bucket = bucket_ref[c]
        start = bucket % CCAP * (PS * HALF)
        for s in range(PS):
            total = even_ref[c * PS + s] + odd_ref[c * PS + s]
            here = pl.multiple_of(start + s * HALF, HALF)
            out_ref[bucket // CCAP, pl.ds(here, HALF)] = total.astype(jnp.bfloat16)
        return carry

    lax.fori_loop(0, coarse_here, finish, 0)


def place_kernel(in_ref, *rest):
    out_ref, peer_ref, start_ref = rest[-3:]
    step = pl.program_id(0)
    peers = in_ref.shape[0]
    per_step, groups = out_ref.shape[0], out_ref.shape[1]
    payload = CCAP * PS * HALF

    @pl.when(step == 0)
    def _():
        for p in range(peers):
            notes = in_ref[p, payload:].astype(jnp.float32)
            which = lax.broadcasted_iota(jnp.int32, notes.shape, 1) // HALF
            for q in range(CCAP):
                place = jnp.max(jnp.where(which == q, notes, -1.0)).astype(jnp.int32)

                @pl.when(place >= 0)
                def _():
                    peer_ref[place] = p
                    start_ref[place] = q * PS * HALF

    perm = block_perm(True)
    low = lane_low(LANES)
    for i in range(per_step):
        s = step * per_step + i
        columns = []
        for g in range(groups):
            blocks = []
            for c in range(GROUP):
                row = g * GROUP + c
                here = pl.multiple_of(start_ref[row] + s * HALF, HALF)
                blocks.append(in_ref[peer_ref[row], pl.ds(here, HALF)])
            columns.append(jnp.concatenate(blocks, axis=0))
        moved = jnp.dot(perm, jnp.concatenate(columns, axis=1), preferred_element_type=jnp.float32)
        moved = moved.astype(jnp.bfloat16)
        for g in range(groups):
            mine = moved[:, g * LANES : (g + 1) * LANES]
            even, odd = mine[0:LANES], mine[LANES:]
            out_ref[i, g, 0:LANES] = jnp.where(low, even, swap_halves(odd))
            out_ref[i, g, LANES:] = jnp.where(low, swap_halves(even), odd)


def whole(shape):
    return pl.BlockSpec(shape, lambda *_: (0,) * len(shape))


def body(a_blocks, p_blocks, a_source, send_list, agg_local, coarse_slot, coarse_target):
    rows, per_row, _ = a_blocks.shape
    peers = lax.axis_size(("px", "py"))
    peers_y = lax.axis_size("py")
    slots = send_list.shape[2]
    coarse_here = rows // AGG
    groups = rows // GROUP
    pairs = (per_row + 3) // 4 * 2
    bf16 = jnp.bfloat16
    smem = pl.BlockSpec(memory_space=pltpu.SMEM)

    a_tiles = as_tiles(a_blocks.transpose(1, 0, 2))
    p_tiles = as_tiles(p_blocks)
    hbm = pl.BlockSpec(memory_space=pltpu.HBM)
    outgoing, own = pl.pallas_call(
        pack_kernel,
        in_specs=[hbm, hbm],
        out_specs=[whole((peers * slots, HALF, LANES)), hbm],
        out_shape=[
            jax.ShapeDtypeStruct((peers * slots, HALF, LANES), bf16),
            jax.ShapeDtypeStruct((rows, HALF, LANES), bf16),
        ],
        scratch_shapes=[
            pltpu.SMEM((slots, peers), jnp.int32),
            pltpu.VMEM((groups, KROWS, LANES), bf16),
            pltpu.VMEM((rows + 1, HALF, LANES), bf16),
            pltpu.SemaphoreType.DMA((groups // 2,)),
            pltpu.SemaphoreType.DMA,
            pltpu.SemaphoreType.DMA,
        ],
        compiler_params=pltpu.CompilerParams(vmem_limit_bytes=60 * MIB),
    )(send_list[0].T, p_tiles)
    arrived = lax.all_to_all(
        outgoing.reshape(peers, slots, HALF, LANES), ("px", "py"), split_axis=0, concat_axis=0, tiled=True
    ).reshape(peers * slots, HALF, LANES)

    sums = coarse_here * PS
    room = groups * LIST + STAGE
    local, tiles, meta, count = pl.pallas_call(
        functools.partial(project_kernel, peers * slots),
        grid=(groups,),
        in_specs=[
            whole((per_row, rows)),
            whole((per_row, rows)),
            whole((1, rows)),
            pl.BlockSpec((per_row, 1, KROWS, LANES), lambda g: (0, g, 0, 0)),
            pl.BlockSpec((1, KROWS, LANES), lambda g: (g, 0, 0)),
            whole((rows, HALF, LANES)),
        ],
        out_specs=[whole((PIECES * sums, HALF, LANES)), hbm, smem, smem],
        out_shape=[
            jax.ShapeDtypeStruct((PIECES * sums, HALF, LANES), jnp.float32),
            jax.ShapeDtypeStruct((PIECES, room, B, LANES), bf16),
            jax.ShapeDtypeStruct((2 * PIECES, room), jnp.int32),
            jax.ShapeDtypeStruct((PIECES,), jnp.int32),
        ],
        scratch_shapes=[
            pltpu.VMEM((GROUP * B, 2 * KROWS), bf16),
            pltpu.VMEM((rows + 1, B, LANES), bf16),
            pltpu.VMEM((rows + 1, B, LANES), bf16),
            pltpu.VMEM((PIECES * sums, HALF, LANES), jnp.float32),
            pltpu.VMEM((PIECES * LIST, B, LANES), bf16),
            pltpu.VMEM((PIECES * LIST, B, LANES), bf16),
            pltpu.VMEM((PIECES, STAGE, B, LANES), bf16),
            pltpu.VMEM((2, per_row, rows), jnp.int32),
            pltpu.SMEM((2, per_row, rows), jnp.int32),
            pltpu.SMEM((2, PIECES * LIST), jnp.int32),
            pltpu.SMEM((PIECES,), jnp.int32),
            pltpu.SMEM((PIECES,), jnp.int32),
            pltpu.SemaphoreType.DMA,
            pltpu.SemaphoreType.DMA((PIECES, STAGE // CHUNK)),
        ],
        compiler_params=pltpu.CompilerParams(vmem_limit_bytes=58 * MIB),
        cost_estimate=pl.CostEstimate(
            flops=4 * 512 * 512 * 128 * pairs * groups, bytes_accessed=45_000_000, transcendentals=0
        ),
    )(a_source.T, coarse_slot.T, agg_local.reshape(1, rows), a_tiles, p_tiles, own)

    piece_rows = CCAP * PS * HALF + 16
    received = []
    for part in range(PIECES):
        sent = pl.pallas_call(
            functools.partial(combine_kernel, part),
            in_specs=[smem, smem, smem, whole((peers * slots, HALF, LANES)), hbm, hbm],
            out_specs=whole((peers_y, piece_rows, LANES)),
            out_shape=jax.ShapeDtypeStruct((peers_y, piece_rows, LANES), bf16),
            scratch_shapes=[
                pltpu.VMEM((peers * slots + 1, B, LANES), bf16),
                pltpu.VMEM((sums + 1, HALF, LANES), jnp.float32),
                pltpu.VMEM((sums + 1, HALF, LANES), jnp.float32),
                pltpu.VMEM((RING, CHUNK, B, LANES), bf16),
                pltpu.SMEM((coarse_here,), jnp.int32),
                pltpu.SMEM((peers_y * CCAP,), jnp.int32),
                pltpu.SMEM((peers_y,), jnp.int32),
                pltpu.SemaphoreType.DMA,
                pltpu.SemaphoreType.DMA((RING,)),
            ],
            compiler_params=pltpu.CompilerParams(vmem_limit_bytes=56 * MIB),
            cost_estimate=pl.CostEstimate(flops=4_000_000_000, bytes_accessed=8_000_000, transcendentals=0),
        )(meta, count, coarse_target, arrived, local, tiles)
        received.append(lax.all_to_all(sent, "py", split_axis=0, concat_axis=0, tiled=True))

    per_step = 3
    out_groups = coarse_here // GROUP
    placed = None
    for part in range(PIECES):
        first = part * PS // per_step
        placed = pl.pallas_call(
            place_kernel,
            grid=(PS // per_step,),
            in_specs=[whole((peers_y, piece_rows, LANES))] + ([hbm] if part else []),
            out_specs=pl.BlockSpec((per_step, out_groups, KROWS, LANES), lambda s, first=first: (first + s, 0, 0, 0)),
            out_shape=jax.ShapeDtypeStruct((S, out_groups, KROWS, LANES), bf16),
            scratch_shapes=[pltpu.SMEM((coarse_here,), jnp.int32), pltpu.SMEM((coarse_here,), jnp.int32)],
            input_output_aliases={1: 0} if part else {},
            compiler_params=pltpu.CompilerParams(vmem_limit_bytes=24 * MIB),
            cost_estimate=pl.CostEstimate(flops=1_000_000_000, bytes_accessed=3_000_000, transcendentals=0),
        )(received[part], *([placed] if part else []))
    return from_tiles(placed).transpose(1, 0, 2)


def solution(mesh):
    rows = ("px", "py")
    in_specs = (
        P(rows, None, None),
        P(rows, None),
        P(rows, None),
        P(rows, None, None),
        P(rows),
        P(rows, None),
        P(rows),
    )
    return jax.shard_map(body, mesh=mesh, in_specs=in_specs, out_specs=P(rows, None, None), check_vma=False)
```

```python
import functools

import jax
import jax.numpy as jnp
from jax import lax
from jax.experimental import pallas as pl
from jax.experimental.pallas import tpu as pltpu
from jax.sharding import PartitionSpec as P

B = 64
FLAT = B * B
LANES = 128
HALF = B // 2
S = 27
AGG = 6
CCAP = 2
GROUP = 8
TILES = FLAT // LANES
KROWS = GROUP * TILES
PIECES = 1
PS = S // PIECES
CHUNK = 32
PEERS = 8
TURN = 8
LIST = 128
STAGE = LIST + 2 * CHUNK
SRC_BITS = 7
PLACE_BITS = 10
FLAG_BIT = 30
RING = 4
MIB = 1 << 20


def lane_low(rows):
    return lax.broadcasted_iota(jnp.int32, (rows, LANES), 1) < B


def swap_halves(x):
    return pltpu.roll(x, B, 1)


def as_tiles(x):
    lead, rows = x.shape[:-2], x.shape[-2]
    split = x.reshape(*lead, rows // GROUP, GROUP, TILES, LANES)
    return jnp.swapaxes(split, -3, -2).reshape(*lead, rows // GROUP, KROWS, LANES)


def from_tiles(x):
    lead, groups = x.shape[:-3], x.shape[-3]
    split = x.reshape(*lead, groups, TILES, GROUP, LANES)
    return jnp.swapaxes(split, -3, -2).reshape(*lead, groups * GROUP, FLAT)


def block_perm(transposed):
    block_axis, tile_axis = (1, 0) if transposed else (0, 1)
    shape = (KROWS, KROWS)
    block_row = lax.broadcasted_iota(jnp.int32, shape, block_axis)
    tile_row = lax.broadcasted_iota(jnp.int32, shape, tile_axis)
    same_r = (block_row // HALF) == (tile_row % GROUP)
    want = 2 * ((tile_row % LANES) // GROUP) + tile_row // LANES
    same_j = (block_row % HALF) == want
    return jnp.where(same_r & same_j, 1.0, 0.0).astype(jnp.bfloat16)


def pack_kernel(
    send_hbm, p_hbm, out_hbm, own_hbm, send_ref, p_ref, table_ref, out_ref, sems, send_sem, own_sem, out_sems
):
    groups = p_ref.shape[0]
    rows = groups * GROUP
    slots, peers = send_ref.shape
    get_send = pltpu.make_async_copy(send_hbm, send_ref, send_sem)
    get_send.start()

    def get(g):
        return pltpu.make_async_copy(p_hbm.at[pl.ds(g, 2)], p_ref.at[pl.ds(g, 2)], sems.at[g // 2])

    for g in range(0, groups, 2):
        get(g).start()
    perm = block_perm(False)
    low = lane_low(LANES)

    def to_blocks(g):
        top, bottom = p_ref[g, 0:LANES, :], p_ref[g, LANES:KROWS, :]
        even = jnp.where(low, top, swap_halves(bottom))
        odd = jnp.where(low, swap_halves(top), bottom)
        return jnp.concatenate([even, odd], axis=0)

    for g in range(0, groups, 2):
        get(g).wait()
        both = jnp.concatenate([to_blocks(g), to_blocks(g + 1)], axis=1)
        blocks = jnp.dot(perm, both, preferred_element_type=jnp.float32).astype(jnp.bfloat16)
        for h in range(2):
            piece = blocks[:, h * LANES : (h + 1) * LANES].reshape(GROUP, HALF, LANES)
            table_ref[pl.ds((g + h) * GROUP, GROUP)] = piece
    put_own = pltpu.make_async_copy(table_ref.at[pl.ds(0, rows)], own_hbm, own_sem)
    put_own.start()
    table_ref[rows] = jnp.zeros((HALF, LANES), jnp.bfloat16)
    get_send.wait()

    def fill(peer, carry):
        for slot in range(slots):
            wanted = send_ref[slot, peer]
            out_ref[peer * slots + slot] = table_ref[jnp.where(wanted < 0, rows, wanted)]
        return carry

    def put(i):
        span = pl.ds(i * PEERS * slots, PEERS * slots)
        return pltpu.make_async_copy(out_ref.at[span], out_hbm.at[span], out_sems.at[i])

    for i in range(peers // PEERS):
        lax.fori_loop(i * PEERS, (i + 1) * PEERS, fill, 0, unroll=2)
        put(i).start()
    put_own.wait()
    for i in range(peers // PEERS):
        put(i).wait()


def fold(value, low):
    top, bottom = value[0:HALF], value[HALF:]
    return jnp.where(low, top, swap_halves(bottom)), jnp.where(low, swap_halves(top), bottom)


def project_kernel(
    ghosts, source_ref, slot_ref, agg_ref, a_ref, p_ref, own_ref, sum_ref, tiles_hbm, meta_ref, count_ref,
    left_ref, first_ref, second_ref, odd_ref, even_tiles, odd_tiles, stage_ref,
    words_vec, words_ref, here_ref, done_ref, flying_ref, words_sem, sems,
):
    step = pl.program_id(0)
    last = pl.num_programs(0) - 1
    per_row, rows = source_ref.shape
    pairs = (per_row + 3) // 4 * 2
    sums = sum_ref.shape[0] // PIECES
    low_half, low_all = lane_low(HALF), lane_low(B)
    zero_all = jnp.zeros((B, LANES), jnp.bfloat16)

    @pl.when(step == 0)
    def _():
        source, slot = source_ref[...], slot_ref[...]
        part = (slot >= PS).astype(jnp.int32)
        for i in range(2, PIECES):
            part += (slot >= i * PS).astype(jnp.int32)
        place = agg_ref[...] * PS + slot - part * PS
        ghost = (source >= rows).astype(jnp.int32)
        words_vec[0] = ((part * sums + place) << SRC_BITS) + jnp.minimum(source, rows)
        words_vec[1] = (ghost << FLAG_BIT) + (jnp.maximum(source - rows, 0) << PLACE_BITS) + place
        load = pltpu.make_async_copy(words_vec, words_ref, words_sem)
        load.start()
        for i in range(PIECES):
            done_ref[i] = 0
            flying_ref[i] = 0

        def expand(i, carry):
            block = own_ref[i]
            turned = swap_halves(block)
            zero = jnp.zeros((HALF, LANES), jnp.bfloat16)
            first_ref[i, 0:HALF] = jnp.where(low_half, block, zero)
            first_ref[i, HALF:] = jnp.where(low_half, turned, zero)
            second_ref[i, 0:HALF] = jnp.where(low_half, zero, turned)
            second_ref[i, HALF:] = jnp.where(low_half, zero, block)
            return carry

        lax.fori_loop(0, rows, expand, 0, unroll=8)
        first_ref[rows] = zero_all
        second_ref[rows] = zero_all

        def clear(i, carry):
            for part in range(PIECES):
                sum_ref[part * sums + i] = jnp.zeros((HALF, LANES), jnp.float32)
                odd_ref[part * sums + i] = jnp.zeros((HALF, LANES), jnp.float32)
            return carry

        lax.fori_loop(0, sums, clear, 0, unroll=4)
        load.wait()

    flipped = p_ref[0].T
    row_of = lax.broadcasted_iota(jnp.int32, (B, KROWS), 1) % GROUP
    zero = jnp.zeros((B, KROWS), jnp.bfloat16)
    for r in range(GROUP):
        mine = row_of == r
        left_ref[r * B : (r + 1) * B, 0:KROWS] = jnp.where(mine, flipped[0:B], zero)
        left_ref[r * B : (r + 1) * B, KROWS:] = jnp.where(mine, flipped[B:], zero)
    low = lane_low(KROWS)

    def pair_of(pair):
        first = a_ref[2 * pair, 0]
        second = a_ref[min(2 * pair + 1, per_row - 1), 0]
        even = jnp.where(low, first, swap_halves(second))
        odd = jnp.where(low, swap_halves(first), second)
        return jnp.concatenate([even, odd], axis=0)

    counts = [jnp.int32(0), jnp.int32(0)]
    for pair in range(0, pairs, 2):
        right = jnp.concatenate([pair_of(pair), pair_of(pair + 1)], axis=1)
        both = jnp.dot(left_ref[...], right, preferred_element_type=jnp.float32).astype(jnp.bfloat16)
        for r in range(GROUP):
            row = step * GROUP + r
            moving = both[r * B : (r + 1) * B]
            weights, targets = [], []
            for h in range(2):
                tile = moving[:, h * LANES : (h + 1) * LANES]
                halves = []
                for parity, table, listed in ((0, first_ref, even_tiles), (1, second_ref, odd_tiles)):
                    k = 2 * (pair + h) + parity
                    if k >= per_row:
                        halves.append(zero_all)
                        targets.append(None)
                        continue
                    word = words_ref[0, k, row]
                    halves.append(table[word & ((1 << SRC_BITS) - 1)])
                    targets.append(word >> SRC_BITS)
                    if k > 0:
                        at = counts[parity]
                        note = words_ref[1, k, row]
                        listed[at] = tile
                        here_ref[parity, at] = note
                        counts[parity] = at + (note >> FLAG_BIT)
                filled = jnp.concatenate(halves, axis=0)
                blank = jnp.zeros_like(filled)
                weights.append(jnp.concatenate([filled, blank] if h == 0 else [blank, filled], axis=1))
            value = jnp.dot(moving, jnp.concatenate(weights, axis=0), preferred_element_type=jnp.float32)
            for h in range(2):
                even, odd = fold(value[:, h * LANES : (h + 1) * LANES], low_half)
                sum_ref[targets[2 * h]] += even
                if targets[2 * h + 1] is not None:
                    odd_ref[targets[2 * h + 1]] += odd

    no_entry = (ghosts << PLACE_BITS) + sums
    for part in range(PIECES):
        even_count, odd_count = counts
        after = jnp.maximum(even_count, odd_count)
        before = done_ref[part]
        chunks = lax.div(after + CHUNK - 1, CHUNK) + jnp.where(step == last, 1, 0)

        def copy(i, start, part=part):
            return pltpu.make_async_copy(
                stage_ref.at[part, pl.ds(i * CHUNK, CHUNK)],
                tiles_hbm.at[part, pl.ds(start + i * CHUNK, CHUNK)],
                sems.at[part, i],
            )

        def finish(i, carry, copy=copy):
            copy(i, 0).wait()
            return carry

        lax.fori_loop(0, flying_ref[part], finish, 0)

        def merge(turn, carry, part=part, even_count=even_count, odd_count=odd_count, before=before):
            for j in range(TURN):
                i = turn * TURN + j
                end = part * LIST + jnp.minimum(i, LIST - 1)
                even_at = jnp.where(low_all, i, STAGE) < even_count
                odd_at = jnp.where(low_all, STAGE, i) < odd_count
                tile = jnp.where(even_at, even_tiles[end], zero_all)
                stage_ref[part, i] = jnp.where(odd_at, odd_tiles[end], tile)
                meta_ref[2 * part, before + i] = jnp.where(i < even_count, here_ref[0, end], no_entry)
                meta_ref[2 * part + 1, before + i] = jnp.where(i < odd_count, here_ref[1, end], no_entry)
            return carry

        turns = jnp.where(step == last, chunks * (CHUNK // TURN), (after + TURN - 1) >> 3)
        lax.fori_loop(0, turns, merge, 0)

        def send(i, carry, copy=copy, before=before):
            copy(i, before).start()
            return carry

        lax.fori_loop(0, chunks, send, 0)
        flying_ref[part] = chunks
        done_ref[part] = before + after

    @pl.when(step == last)
    def _():
        def total(i, carry):
            for part in range(PIECES):
                sum_ref[part * sums + i] += odd_ref[part * sums + i]
            return carry

        lax.fori_loop(0, sums, total, 0, unroll=4)
        for part in range(PIECES):
            count_ref[part] = lax.div(done_ref[part] + CHUNK - 1, CHUNK)

            def drain(i, carry, part=part):
                pltpu.make_async_copy(
                    stage_ref.at[part, pl.ds(i * CHUNK, CHUNK)],
                    tiles_hbm.at[part, pl.ds(i * CHUNK, CHUNK)],
                    sems.at[part, i],
                ).wait()
                return carry

            lax.fori_loop(0, flying_ref[part], drain, 0)


def combine_kernel(
    part, meta_ref, count_ref, target_ref, ghost_hbm, sum_hbm, tiles_hbm, out_hbm,
    ghost_ref, even_ref, odd_ref, tiles_ref, out_ref, bucket_ref, place_ref, per_peer_ref,
    ghost_sem, sum_sem, note_sem, sems, out_sems,
):
    ghosts = ghost_hbm.shape[0]
    coarse_here = target_ref.shape[0]
    sums = coarse_here * PS
    peers = out_ref.shape[0]
    chunks = count_ref[part]
    low_half = lane_low(HALF)
    zero_half = jnp.zeros((HALF, LANES), jnp.bfloat16)
    load_sums = pltpu.make_async_copy(sum_hbm.at[pl.ds(part * sums, sums)], even_ref.at[pl.ds(0, sums)], sum_sem)
    load_sums.start()
    load_ghosts = pltpu.make_async_copy(ghost_hbm, ghost_ref.at[pl.ds(0, ghosts)], ghost_sem)
    load_ghosts.start()

    def fetch(i):
        slot = lax.rem(i, RING)
        return pltpu.make_async_copy(tiles_hbm.at[part, pl.ds(i * CHUNK, CHUNK)], tiles_ref.at[slot], sems.at[slot])

    for i in range(RING - 1):

        @pl.when(i < chunks)
        def _():
            fetch(i).start()

    ghost_ref[ghosts] = zero_half

    def clear(i, carry):
        odd_ref[i] = jnp.zeros((HALF, LANES), jnp.float32)
        return carry

    lax.fori_loop(0, sums, clear, 0, unroll=8)

    for p in range(peers):
        per_peer_ref[p] = 0
        for q in range(CCAP):
            place_ref[p * CCAP + q] = -1

    def assign(c, carry):
        target = target_ref[c]
        peer = lax.rem(lax.div(target, coarse_here), peers)
        bucket = peer * CCAP + per_peer_ref[peer]
        per_peer_ref[peer] = per_peer_ref[peer] + 1
        bucket_ref[c] = bucket
        place_ref[bucket] = lax.rem(target, coarse_here)
        return carry

    lax.fori_loop(0, coarse_here, assign, 0)
    payload = CCAP * PS * HALF
    second_slot = lax.broadcasted_iota(jnp.int32, (out_ref.shape[1] - payload, LANES), 1) // HALF % CCAP

    def note(p, carry):
        value = jnp.full(second_slot.shape, -1, jnp.int32)
        for q in range(CCAP):
            value = jnp.where(second_slot == q, place_ref[p * CCAP + q], value)
        out_ref[p, payload:] = value.astype(jnp.float32).astype(jnp.bfloat16)
        return carry

    lax.fori_loop(0, peers, note, 0)
    notes = pl.ds(payload, out_ref.shape[1] - payload)
    put_notes = pltpu.make_async_copy(out_ref.at[:, notes], out_hbm.at[:, notes], note_sem)
    put_notes.start()
    load_ghosts.wait()
    load_sums.wait()

    def work(i, carry):
        @pl.when(i + RING - 1 < chunks)
        def _():
            fetch(i + RING - 1).start()

        fetch(i).wait()
        slot = lax.rem(i, RING)
        for j in range(0, CHUNK, 2):
            weights, targets = [], []
            for h in range(2):
                at = i * CHUNK + j + h
                even, odd = meta_ref[2 * part, at], meta_ref[2 * part + 1, at]
                first = ghost_ref[(even >> PLACE_BITS) & ((1 << FLAG_BIT - PLACE_BITS) - 1)]
                second = ghost_ref[(odd >> PLACE_BITS) & ((1 << FLAG_BIT - PLACE_BITS) - 1)]
                targets += [even & ((1 << PLACE_BITS) - 1), odd & ((1 << PLACE_BITS) - 1)]
                filled = jnp.concatenate(
                    [
                        jnp.where(low_half, first, zero_half),
                        jnp.where(low_half, swap_halves(first), zero_half),
                        jnp.where(low_half, zero_half, swap_halves(second)),
                        jnp.where(low_half, zero_half, second),
                    ],
                    axis=0,
                )
                blank = jnp.zeros_like(filled)
                weights.append(jnp.concatenate([filled, blank] if h == 0 else [blank, filled], axis=1))
            moving = jnp.concatenate([tiles_ref[slot, j], tiles_ref[slot, j + 1]], axis=1)
            value = jnp.dot(moving, jnp.concatenate(weights, axis=0), preferred_element_type=jnp.float32)
            for h in range(2):
                even, odd = fold(value[:, h * LANES : (h + 1) * LANES], low_half)
                even_ref[targets[2 * h]] += even
                odd_ref[targets[2 * h + 1]] += odd
        return carry

    lax.fori_loop(0, chunks, work, 0)

    def put(c):
        bucket = bucket_ref[c]
        span = pl.ds(pl.multiple_of(lax.rem(bucket, CCAP) * (PS * HALF), HALF), PS * HALF)
        peer = lax.div(bucket, CCAP)
        return pltpu.make_async_copy(out_ref.at[peer, span], out_hbm.at[peer, span], out_sems.at[c])

    def finish(c, carry):
        bucket = bucket_ref[c]
        start = lax.rem(bucket, CCAP) * (PS * HALF)
        peer = lax.div(bucket, CCAP)
        first = c * PS
        for s in range(PS):
            total = even_ref[first + s] + odd_ref[first + s]
            here = pl.multiple_of(start + s * HALF, HALF)
            out_ref[peer, pl.ds(here, HALF)] = total.astype(jnp.bfloat16)
        put(c).start()
        return carry

    lax.fori_loop(0, coarse_here, finish, 0)
    put_notes.wait()
    lax.fori_loop(0, coarse_here, lambda c, carry: (put(c).wait(), carry)[1], 0)


def place_kernel(in_ref, *rest):
    out_ref, peer_ref, start_ref = rest[-3:]
    step = pl.program_id(0)
    peers = in_ref.shape[0]
    per_step, groups = out_ref.shape[0], out_ref.shape[1]
    payload = CCAP * PS * HALF

    @pl.when(step == 0)
    def _():
        for p in range(peers):
            notes = in_ref[p, payload:].astype(jnp.float32)
            which = lax.broadcasted_iota(jnp.int32, notes.shape, 1) // HALF
            for q in range(CCAP):
                place = jnp.max(jnp.where(which == q, notes, -1.0)).astype(jnp.int32)
                entry = jnp.where(place < 0, groups * GROUP, place)
                peer_ref[entry] = p
                start_ref[entry] = q * PS * HALF

    perm = block_perm(True)
    low = lane_low(LANES)
    for i in range(per_step):
        s = step * per_step + i
        columns = []
        for g in range(groups):
            blocks = []
            for c in range(GROUP):
                row = g * GROUP + c
                here = pl.multiple_of(start_ref[row] + s * HALF, HALF)
                blocks.append(in_ref[peer_ref[row], pl.ds(here, HALF)])
            columns.append(jnp.concatenate(blocks, axis=0))
        moved = jnp.dot(perm, jnp.concatenate(columns, axis=1), preferred_element_type=jnp.float32)
        moved = moved.astype(jnp.bfloat16)
        for g in range(groups):
            mine = moved[:, g * LANES : (g + 1) * LANES]
            even, odd = mine[0:LANES], mine[LANES:]
            out_ref[i, g, 0:LANES] = jnp.where(low, even, swap_halves(odd))
            out_ref[i, g, LANES:] = jnp.where(low, swap_halves(even), odd)


def whole(shape):
    return pl.BlockSpec(shape, lambda *_: (0,) * len(shape))


def body(a_blocks, p_blocks, a_source, send_list, agg_local, coarse_slot, coarse_target):
    rows, per_row, _ = a_blocks.shape
    peers = lax.axis_size(("px", "py"))
    peers_y = lax.axis_size("py")
    slots = send_list.shape[2]
    coarse_here = rows // AGG
    groups = rows // GROUP
    pairs = (per_row + 3) // 4 * 2
    bf16 = jnp.bfloat16
    smem = pl.BlockSpec(memory_space=pltpu.SMEM)

    a_tiles = as_tiles(a_blocks.transpose(1, 0, 2))
    p_tiles = as_tiles(p_blocks)
    hbm = pl.BlockSpec(memory_space=pltpu.HBM)
    outgoing, own = pl.pallas_call(
        pack_kernel,
        in_specs=[hbm, hbm],
        out_specs=[hbm, hbm],
        out_shape=[
            jax.ShapeDtypeStruct((peers * slots, HALF, LANES), bf16),
            jax.ShapeDtypeStruct((rows, HALF, LANES), bf16),
        ],
        scratch_shapes=[
            pltpu.SMEM((slots, peers), jnp.int32),
            pltpu.VMEM((groups, KROWS, LANES), bf16),
            pltpu.VMEM((rows + 1, HALF, LANES), bf16),
            pltpu.VMEM((peers * slots, HALF, LANES), bf16),
            pltpu.SemaphoreType.DMA((groups // 2,)),
            pltpu.SemaphoreType.DMA,
            pltpu.SemaphoreType.DMA,
            pltpu.SemaphoreType.DMA((peers // PEERS,)),
        ],
        compiler_params=pltpu.CompilerParams(vmem_limit_bytes=60 * MIB),
    )(send_list[0].T, p_tiles)
    arrived = lax.all_to_all(
        outgoing.reshape(peers, slots, HALF, LANES), ("px", "py"), split_axis=0, concat_axis=0, tiled=True
    ).reshape(peers * slots, HALF, LANES)

    sums = coarse_here * PS
    room = groups * LIST + STAGE
    local, tiles, meta, count = pl.pallas_call(
        functools.partial(project_kernel, peers * slots),
        grid=(groups,),
        in_specs=[
            whole((per_row, rows)),
            whole((per_row, rows)),
            whole((1, rows)),
            pl.BlockSpec((per_row, 1, KROWS, LANES), lambda g: (0, g, 0, 0)),
            pl.BlockSpec((1, KROWS, LANES), lambda g: (g, 0, 0)),
            whole((rows, HALF, LANES)),
        ],
        out_specs=[whole((PIECES * sums, HALF, LANES)), hbm, smem, smem],
        out_shape=[
            jax.ShapeDtypeStruct((PIECES * sums, HALF, LANES), jnp.float32),
            jax.ShapeDtypeStruct((PIECES, room, B, LANES), bf16),
            jax.ShapeDtypeStruct((2 * PIECES, room), jnp.int32),
            jax.ShapeDtypeStruct((PIECES,), jnp.int32),
        ],
        scratch_shapes=[
            pltpu.VMEM((GROUP * B, 2 * KROWS), bf16),
            pltpu.VMEM((rows + 1, B, LANES), bf16),
            pltpu.VMEM((rows + 1, B, LANES), bf16),
            pltpu.VMEM((PIECES * sums, HALF, LANES), jnp.float32),
            pltpu.VMEM((PIECES * LIST, B, LANES), bf16),
            pltpu.VMEM((PIECES * LIST, B, LANES), bf16),
            pltpu.VMEM((PIECES, STAGE, B, LANES), bf16),
            pltpu.VMEM((2, per_row, rows), jnp.int32),
            pltpu.SMEM((2, per_row, rows), jnp.int32),
            pltpu.SMEM((2, PIECES * LIST), jnp.int32),
            pltpu.SMEM((PIECES,), jnp.int32),
            pltpu.SMEM((PIECES,), jnp.int32),
            pltpu.SemaphoreType.DMA,
            pltpu.SemaphoreType.DMA((PIECES, STAGE // CHUNK)),
        ],
        compiler_params=pltpu.CompilerParams(vmem_limit_bytes=63 * MIB),
        cost_estimate=pl.CostEstimate(
            flops=4 * 512 * 512 * 128 * pairs * groups, bytes_accessed=45_000_000, transcendentals=0
        ),
    )(a_source.T, coarse_slot.T, agg_local.reshape(1, rows), a_tiles, p_tiles, own)

    piece_rows = CCAP * PS * HALF + 16
    received = []
    for part in range(PIECES):
        sent = pl.pallas_call(
            functools.partial(combine_kernel, part),
            in_specs=[smem, smem, smem, hbm, hbm, hbm],
            out_specs=hbm,
            out_shape=jax.ShapeDtypeStruct((peers_y, piece_rows, LANES), bf16),
            scratch_shapes=[
                pltpu.VMEM((peers * slots + 1, HALF, LANES), bf16),
                pltpu.VMEM((sums + 1, HALF, LANES), jnp.float32),
                pltpu.VMEM((sums + 1, HALF, LANES), jnp.float32),
                pltpu.VMEM((RING, CHUNK, B, LANES), bf16),
                pltpu.VMEM((peers_y, piece_rows, LANES), bf16),
                pltpu.SMEM((coarse_here,), jnp.int32),
                pltpu.SMEM((peers_y * CCAP,), jnp.int32),
                pltpu.SMEM((peers_y,), jnp.int32),
                pltpu.SemaphoreType.DMA,
                pltpu.SemaphoreType.DMA,
                pltpu.SemaphoreType.DMA,
                pltpu.SemaphoreType.DMA((RING,)),
                pltpu.SemaphoreType.DMA((coarse_here,)),
            ],
            compiler_params=pltpu.CompilerParams(vmem_limit_bytes=56 * MIB),
            cost_estimate=pl.CostEstimate(flops=4_000_000_000, bytes_accessed=8_000_000, transcendentals=0),
        )(meta, count, coarse_target, arrived, local, tiles)
        received.append(lax.all_to_all(sent, "py", split_axis=0, concat_axis=0, tiled=True))

    per_step = 9
    out_groups = coarse_here // GROUP
    placed = None
    for part in range(PIECES):
        first = part * PS // per_step
        placed = pl.pallas_call(
            place_kernel,
            grid=(PS // per_step,),
            in_specs=[whole((peers_y, piece_rows, LANES))] + ([hbm] if part else []),
            out_specs=pl.BlockSpec((per_step, out_groups, KROWS, LANES), lambda s, first=first: (first + s, 0, 0, 0)),
            out_shape=jax.ShapeDtypeStruct((S, out_groups, KROWS, LANES), bf16),
            scratch_shapes=[pltpu.SMEM((coarse_here + 1,), jnp.int32), pltpu.SMEM((coarse_here + 1,), jnp.int32)],
            input_output_aliases={1: 0} if part else {},
            compiler_params=pltpu.CompilerParams(vmem_limit_bytes=24 * MIB),
            cost_estimate=pl.CostEstimate(flops=1_000_000_000, bytes_accessed=3_000_000, transcendentals=0),
        )(received[part], *([placed] if part else []))
    return from_tiles(placed).transpose(1, 0, 2)


def solution(mesh):
    rows = ("px", "py")
    in_specs = (
        P(rows, None, None),
        P(rows, None),
        P(rows, None),
        P(rows, None, None),
        P(rows),
        P(rows, None),
        P(rows),
    )
    return jax.shard_map(body, mesh=mesh, in_specs=in_specs, out_specs=P(rows, None, None), check_vma=False)
```

```python
import functools

import jax
import jax.numpy as jnp
from jax import lax
from jax.experimental import pallas as pl
from jax.experimental.pallas import tpu as pltpu
from jax.sharding import PartitionSpec as P

B = 64
FLAT = B * B
LANES = 128
HALF = B // 2
S = 27
AGG = 6
CCAP = 2
GROUP = 8
TILES = FLAT // LANES
KROWS = GROUP * TILES
PIECES = 1
PS = S // PIECES
CHUNK = 32
PEERS = 8
TURN = 8
LIST = 128
STAGE = LIST + 2 * CHUNK
SRC_BITS = 7
PLACE_BITS = 10
FLAG_BIT = 30
RING = 4
MIB = 1 << 20


def lane_low(rows):
    return lax.broadcasted_iota(jnp.int32, (rows, LANES), 1) < B


def swap_halves(x):
    return pltpu.roll(x, B, 1)


def as_tiles(x):
    lead, rows = x.shape[:-2], x.shape[-2]
    split = x.reshape(*lead, rows // GROUP, GROUP, TILES, LANES)
    return jnp.swapaxes(split, -3, -2).reshape(*lead, rows // GROUP, KROWS, LANES)


def from_tiles(x):
    lead, groups = x.shape[:-3], x.shape[-3]
    split = x.reshape(*lead, groups, TILES, GROUP, LANES)
    return jnp.swapaxes(split, -3, -2).reshape(*lead, groups * GROUP, FLAT)


def block_perm(transposed):
    block_axis, tile_axis = (1, 0) if transposed else (0, 1)
    shape = (KROWS, KROWS)
    block_row = lax.broadcasted_iota(jnp.int32, shape, block_axis)
    tile_row = lax.broadcasted_iota(jnp.int32, shape, tile_axis)
    same_r = (block_row // HALF) == (tile_row % GROUP)
    want = 2 * ((tile_row % LANES) // GROUP) + tile_row // LANES
    same_j = (block_row % HALF) == want
    return jnp.where(same_r & same_j, 1.0, 0.0).astype(jnp.bfloat16)


def pack_kernel(
    send_hbm, p_hbm, out_hbm, own_hbm, send_ref, p_ref, table_ref, out_ref, sems, send_sem, own_sem, out_sems
):
    groups = p_ref.shape[0]
    rows = groups * GROUP
    slots, peers = send_ref.shape
    get_send = pltpu.make_async_copy(send_hbm, send_ref, send_sem)
    get_send.start()

    def get(g):
        return pltpu.make_async_copy(p_hbm.at[pl.ds(g, 2)], p_ref.at[pl.ds(g, 2)], sems.at[g // 2])

    for g in range(0, groups, 2):
        get(g).start()
    perm = block_perm(False)
    low = lane_low(LANES)

    def to_blocks(g):
        top, bottom = p_ref[g, 0:LANES, :], p_ref[g, LANES:KROWS, :]
        even = jnp.where(low, top, swap_halves(bottom))
        odd = jnp.where(low, swap_halves(top), bottom)
        return jnp.concatenate([even, odd], axis=0)

    for g in range(0, groups, 2):
        get(g).wait()
        both = jnp.concatenate([to_blocks(g), to_blocks(g + 1)], axis=1)
        blocks = jnp.dot(perm, both, preferred_element_type=jnp.float32).astype(jnp.bfloat16)
        for h in range(2):
            piece = blocks[:, h * LANES : (h + 1) * LANES].reshape(GROUP, HALF, LANES)
            table_ref[pl.ds((g + h) * GROUP, GROUP)] = piece
    put_own = pltpu.make_async_copy(table_ref.at[pl.ds(0, rows)], own_hbm, own_sem)
    put_own.start()
    table_ref[rows] = jnp.zeros((HALF, LANES), jnp.bfloat16)
    get_send.wait()

    def fill(peer, carry):
        for slot in range(slots):
            wanted = send_ref[slot, peer]
            out_ref[peer * slots + slot] = table_ref[jnp.where(wanted < 0, rows, wanted)]
        return carry

    def put(i):
        span = pl.ds(i * PEERS * slots, PEERS * slots)
        return pltpu.make_async_copy(out_ref.at[span], out_hbm.at[span], out_sems.at[i])

    for i in range(peers // PEERS):
        lax.fori_loop(i * PEERS, (i + 1) * PEERS, fill, 0, unroll=2)
        put(i).start()
    put_own.wait()
    for i in range(peers // PEERS):
        put(i).wait()


def fold(value, low):
    top, bottom = value[0:HALF], value[HALF:]
    return jnp.where(low, top, swap_halves(bottom)), jnp.where(low, swap_halves(top), bottom)


def project_kernel(
    ghosts, source_ref, slot_ref, agg_ref, a_ref, p_ref, own_ref, sum_ref, tiles_hbm, meta_ref, count_ref,
    left_ref, first_ref, second_ref, odd_ref, even_tiles, odd_tiles, stage_ref,
    words_vec, words_ref, here_ref, done_ref, flying_ref, words_sem, sems,
):
    step = pl.program_id(0)
    last = pl.num_programs(0) - 1
    per_row, rows = source_ref.shape
    pairs = (per_row + 3) // 4 * 2
    sums = sum_ref.shape[0] // PIECES
    low_half, low_all = lane_low(HALF), lane_low(B)
    zero_all = jnp.zeros((B, LANES), jnp.bfloat16)

    @pl.when(step == 0)
    def _():
        source, slot = source_ref[...], slot_ref[...]
        part = (slot >= PS).astype(jnp.int32)
        for i in range(2, PIECES):
            part += (slot >= i * PS).astype(jnp.int32)
        place = agg_ref[...] * PS + slot - part * PS
        ghost = (source >= rows).astype(jnp.int32)
        words_vec[0] = ((part * sums + place) << SRC_BITS) + jnp.minimum(source, rows)
        words_vec[1] = (ghost << FLAG_BIT) + (jnp.maximum(source - rows, 0) << PLACE_BITS) + place
        load = pltpu.make_async_copy(words_vec, words_ref, words_sem)
        load.start()
        for i in range(PIECES):
            done_ref[i] = 0
            flying_ref[i] = 0

        def expand(i, carry):
            block = own_ref[i]
            turned = swap_halves(block)
            zero = jnp.zeros((HALF, LANES), jnp.bfloat16)
            first_ref[i, 0:HALF] = jnp.where(low_half, block, zero)
            first_ref[i, HALF:] = jnp.where(low_half, turned, zero)
            second_ref[i, 0:HALF] = jnp.where(low_half, zero, turned)
            second_ref[i, HALF:] = jnp.where(low_half, zero, block)
            return carry

        lax.fori_loop(0, rows, expand, 0, unroll=8)
        first_ref[rows] = zero_all
        second_ref[rows] = zero_all

        def clear(i, carry):
            for part in range(PIECES):
                sum_ref[part * sums + i] = jnp.zeros((HALF, LANES), jnp.float32)
                odd_ref[part * sums + i] = jnp.zeros((HALF, LANES), jnp.float32)
            return carry

        lax.fori_loop(0, sums, clear, 0, unroll=4)
        load.wait()

    flipped = p_ref[0].T
    row_of = lax.broadcasted_iota(jnp.int32, (B, KROWS), 1) % GROUP
    zero = jnp.zeros((B, KROWS), jnp.bfloat16)
    for r in range(GROUP):
        mine = row_of == r
        left_ref[r * B : (r + 1) * B, 0:KROWS] = jnp.where(mine, flipped[0:B], zero)
        left_ref[r * B : (r + 1) * B, KROWS:] = jnp.where(mine, flipped[B:], zero)
    low = lane_low(KROWS)

    def pair_of(pair):
        first = a_ref[2 * pair, 0]
        second = a_ref[min(2 * pair + 1, per_row - 1), 0]
        even = jnp.where(low, first, swap_halves(second))
        odd = jnp.where(low, swap_halves(first), second)
        return jnp.concatenate([even, odd], axis=0)

    counts = [jnp.int32(0), jnp.int32(0)]
    for pair in range(0, pairs, 2):
        right = jnp.concatenate([pair_of(pair), pair_of(pair + 1)], axis=1)
        both = jnp.dot(left_ref[...], right, preferred_element_type=jnp.float32).astype(jnp.bfloat16)
        for r in range(GROUP):
            row = step * GROUP + r
            moving = both[r * B : (r + 1) * B]
            for h in range(2):
                tile = moving[:, h * LANES : (h + 1) * LANES]
                halves, targets = [], []
                for parity, table, listed in ((0, first_ref, even_tiles), (1, second_ref, odd_tiles)):
                    k = 2 * (pair + h) + parity
                    if k >= per_row:
                        halves.append(zero_all)
                        targets.append(None)
                        continue
                    word = words_ref[0, k, row]
                    halves.append(table[word & ((1 << SRC_BITS) - 1)])
                    targets.append(word >> SRC_BITS)
                    if k > 0:
                        at = counts[parity]
                        note = words_ref[1, k, row]
                        listed[at] = tile
                        here_ref[parity, at] = note
                        counts[parity] = at + (note >> FLAG_BIT)
                filled = jnp.concatenate(halves, axis=0)
                value = jnp.dot(tile, filled, preferred_element_type=jnp.float32)
                even, odd = fold(value, low_half)
                sum_ref[targets[0]] += even
                if targets[1] is not None:
                    odd_ref[targets[1]] += odd

    no_entry = (ghosts << PLACE_BITS) + sums
    for part in range(PIECES):
        even_count, odd_count = counts
        after = jnp.maximum(even_count, odd_count)
        before = done_ref[part]
        chunks = lax.div(after + CHUNK - 1, CHUNK) + jnp.where(step == last, 1, 0)

        def copy(i, start, part=part):
            return pltpu.make_async_copy(
                stage_ref.at[part, pl.ds(i * CHUNK, CHUNK)],
                tiles_hbm.at[part, pl.ds(start + i * CHUNK, CHUNK)],
                sems.at[part, i],
            )

        def finish(i, carry, copy=copy):
            copy(i, 0).wait()
            return carry

        lax.fori_loop(0, flying_ref[part], finish, 0)

        def merge(turn, carry, part=part, even_count=even_count, odd_count=odd_count, before=before):
            for j in range(TURN):
                i = turn * TURN + j
                end = part * LIST + jnp.minimum(i, LIST - 1)
                even_at = jnp.where(low_all, i, STAGE) < even_count
                odd_at = jnp.where(low_all, STAGE, i) < odd_count
                tile = jnp.where(even_at, even_tiles[end], zero_all)
                stage_ref[part, i] = jnp.where(odd_at, odd_tiles[end], tile)
                meta_ref[2 * part, before + i] = jnp.where(i < even_count, here_ref[0, end], no_entry)
                meta_ref[2 * part + 1, before + i] = jnp.where(i < odd_count, here_ref[1, end], no_entry)
            return carry

        turns = jnp.where(step == last, chunks * (CHUNK // TURN), (after + TURN - 1) >> 3)
        lax.fori_loop(0, turns, merge, 0)

        def send(i, carry, copy=copy, before=before):
            copy(i, before).start()
            return carry

        lax.fori_loop(0, chunks, send, 0)
        flying_ref[part] = chunks
        done_ref[part] = before + after

    @pl.when(step == last)
    def _():
        def total(i, carry):
            for part in range(PIECES):
                sum_ref[part * sums + i] += odd_ref[part * sums + i]
            return carry

        lax.fori_loop(0, sums, total, 0, unroll=4)
        for part in range(PIECES):
            count_ref[part] = lax.div(done_ref[part] + CHUNK - 1, CHUNK)

            def drain(i, carry, part=part):
                pltpu.make_async_copy(
                    stage_ref.at[part, pl.ds(i * CHUNK, CHUNK)],
                    tiles_hbm.at[part, pl.ds(i * CHUNK, CHUNK)],
                    sems.at[part, i],
                ).wait()
                return carry

            lax.fori_loop(0, flying_ref[part], drain, 0)


def combine_kernel(
    part, peers, meta_ref, count_ref, target_ref, me_ref, ghost_hbm, sum_hbm, tiles_hbm, *rest
):
    outs = rest[:peers]
    (
        ghost_ref, even_ref, odd_ref, tiles_ref, out_ref, bucket_ref, place_ref, per_peer_ref,
        ghost_sem, sum_sem, note_sems, sems, out_sems,
    ) = rest[peers:]
    me = me_ref[0]
    ghosts = ghost_hbm.shape[0]
    coarse_here = target_ref.shape[0]
    sums = coarse_here * PS
    chunks = count_ref[part]
    low_half = lane_low(HALF)
    zero_half = jnp.zeros((HALF, LANES), jnp.bfloat16)
    load_sums = pltpu.make_async_copy(sum_hbm.at[pl.ds(part * sums, sums)], even_ref.at[pl.ds(0, sums)], sum_sem)
    load_sums.start()
    load_ghosts = pltpu.make_async_copy(ghost_hbm, ghost_ref.at[pl.ds(0, ghosts)], ghost_sem)
    load_ghosts.start()

    def fetch(i):
        slot = lax.rem(i, RING)
        return pltpu.make_async_copy(tiles_hbm.at[part, pl.ds(i * CHUNK, CHUNK)], tiles_ref.at[slot], sems.at[slot])

    for i in range(RING - 1):

        @pl.when(i < chunks)
        def _():
            fetch(i).start()

    ghost_ref[ghosts] = zero_half

    def clear(i, carry):
        odd_ref[i] = jnp.zeros((HALF, LANES), jnp.float32)
        return carry

    lax.fori_loop(0, sums, clear, 0, unroll=8)

    for p in range(peers):
        per_peer_ref[p] = 0
        for q in range(CCAP):
            place_ref[p * CCAP + q] = -1

    def assign(c, carry):
        target = target_ref[c]
        peer = lax.rem(lax.div(target, coarse_here), peers)
        bucket = peer * CCAP + per_peer_ref[peer]
        per_peer_ref[peer] = per_peer_ref[peer] + 1
        bucket_ref[c] = bucket
        place_ref[bucket] = lax.rem(target, coarse_here)
        return carry

    lax.fori_loop(0, coarse_here, assign, 0)
    payload = CCAP * PS * HALF
    second_slot = lax.broadcasted_iota(jnp.int32, (out_ref.shape[1] - payload, LANES), 1) // HALF % CCAP

    def note(p, carry):
        value = jnp.full(second_slot.shape, -1, jnp.int32)
        for q in range(CCAP):
            value = jnp.where(second_slot == q, place_ref[(p ^ me) * CCAP + q], value)
        out_ref[p, payload:] = value.astype(jnp.float32).astype(jnp.bfloat16)
        return carry

    lax.fori_loop(0, peers, note, 0)
    notes = pl.ds(payload, out_ref.shape[1] - payload)

    def put_notes(d):
        return pltpu.make_async_copy(out_ref.at[d, notes], outs[d].at[notes], note_sems.at[d])

    for d in range(peers):
        put_notes(d).start()
    load_ghosts.wait()
    load_sums.wait()

    def work(i, carry):
        @pl.when(i + RING - 1 < chunks)
        def _():
            fetch(i + RING - 1).start()

        fetch(i).wait()
        slot = lax.rem(i, RING)
        for j in range(CHUNK):
            at = i * CHUNK + j
            even, odd = meta_ref[2 * part, at], meta_ref[2 * part + 1, at]
            first = ghost_ref[(even >> PLACE_BITS) & ((1 << FLAG_BIT - PLACE_BITS) - 1)]
            second = ghost_ref[(odd >> PLACE_BITS) & ((1 << FLAG_BIT - PLACE_BITS) - 1)]
            filled = jnp.concatenate(
                [
                    jnp.where(low_half, first, zero_half),
                    jnp.where(low_half, swap_halves(first), zero_half),
                    jnp.where(low_half, zero_half, swap_halves(second)),
                    jnp.where(low_half, zero_half, second),
                ],
                axis=0,
            )
            value = jnp.dot(tiles_ref[slot, j], filled, preferred_element_type=jnp.float32)
            to_even, to_odd = fold(value, low_half)
            even_ref[even & ((1 << PLACE_BITS) - 1)] += to_even
            odd_ref[odd & ((1 << PLACE_BITS) - 1)] += to_odd
        return carry

    lax.fori_loop(0, chunks, work, 0)

    def put(c, d, start):
        span = pl.ds(start, PS * HALF)
        return pltpu.make_async_copy(out_ref.at[d, span], outs[d].at[span], out_sems.at[c])

    def finish(c, carry):
        bucket = bucket_ref[c]
        start = pl.multiple_of(lax.rem(bucket, CCAP) * (PS * HALF), HALF)
        offset = lax.div(bucket, CCAP) ^ me
        first = c * PS
        for s in range(PS):
            total = even_ref[first + s] + odd_ref[first + s]
            out_ref[offset, pl.ds(pl.multiple_of(start + s * HALF, HALF), HALF)] = total.astype(jnp.bfloat16)
        for d in range(peers):

            @pl.when(offset == d)
            def _():
                put(c, d, start).start()

        return carry

    lax.fori_loop(0, coarse_here, finish, 0)
    for d in range(peers):
        put_notes(d).wait()
    lax.fori_loop(0, coarse_here, lambda c, carry: (put(c, 0, 0).wait(), carry)[1], 0)


def place_kernel(peers, *refs):
    parts = refs[:peers]
    out_ref, in_ref, peer_ref, start_ref, sems = refs[peers:]
    step = pl.program_id(0)
    per_step, groups = out_ref.shape[0], out_ref.shape[1]
    payload = CCAP * PS * HALF

    @pl.when(step == 0)
    def _():
        loads = [pltpu.make_async_copy(parts[d], in_ref.at[d], sems.at[d]) for d in range(peers)]
        for load in loads:
            load.start()
        for p in range(peers):
            loads[p].wait()
            notes = in_ref[p, payload:].astype(jnp.float32)
            which = lax.broadcasted_iota(jnp.int32, notes.shape, 1) // HALF
            for q in range(CCAP):
                place = jnp.max(jnp.where(which == q, notes, -1.0)).astype(jnp.int32)
                entry = jnp.where(place < 0, groups * GROUP, place)
                peer_ref[entry] = p
                start_ref[entry] = q * PS * HALF

    perm = block_perm(True)
    low = lane_low(LANES)
    for i in range(per_step):
        s = step * per_step + i
        columns = []
        for g in range(groups):
            blocks = []
            for c in range(GROUP):
                row = g * GROUP + c
                here = pl.multiple_of(start_ref[row] + s * HALF, HALF)
                blocks.append(in_ref[peer_ref[row], pl.ds(here, HALF)])
            columns.append(jnp.concatenate(blocks, axis=0))
        moved = jnp.dot(perm, jnp.concatenate(columns, axis=1), preferred_element_type=jnp.float32)
        moved = moved.astype(jnp.bfloat16)
        for g in range(groups):
            mine = moved[:, g * LANES : (g + 1) * LANES]
            even, odd = mine[0:LANES], mine[LANES:]
            out_ref[i, g, 0:LANES] = jnp.where(low, even, swap_halves(odd))
            out_ref[i, g, LANES:] = jnp.where(low, swap_halves(even), odd)


def whole(shape):
    return pl.BlockSpec(shape, lambda *_: (0,) * len(shape))


def body(a_blocks, p_blocks, a_source, send_list, agg_local, coarse_slot, coarse_target):
    rows, per_row, _ = a_blocks.shape
    peers = lax.axis_size(("px", "py"))
    peers_y = lax.axis_size("py")
    slots = send_list.shape[2]
    coarse_here = rows // AGG
    groups = rows // GROUP
    pairs = (per_row + 3) // 4 * 2
    bf16 = jnp.bfloat16
    smem = pl.BlockSpec(memory_space=pltpu.SMEM)

    a_tiles = as_tiles(a_blocks.transpose(1, 0, 2))
    p_tiles = as_tiles(p_blocks)
    hbm = pl.BlockSpec(memory_space=pltpu.HBM)
    outgoing, own = pl.pallas_call(
        pack_kernel,
        in_specs=[hbm, hbm],
        out_specs=[hbm, hbm],
        out_shape=[
            jax.ShapeDtypeStruct((peers * slots, HALF, LANES), bf16),
            jax.ShapeDtypeStruct((rows, HALF, LANES), bf16),
        ],
        scratch_shapes=[
            pltpu.SMEM((slots, peers), jnp.int32),
            pltpu.VMEM((groups, KROWS, LANES), bf16),
            pltpu.VMEM((rows + 1, HALF, LANES), bf16),
            pltpu.VMEM((peers * slots, HALF, LANES), bf16),
            pltpu.SemaphoreType.DMA((groups // 2,)),
            pltpu.SemaphoreType.DMA,
            pltpu.SemaphoreType.DMA,
            pltpu.SemaphoreType.DMA((peers // PEERS,)),
        ],
        compiler_params=pltpu.CompilerParams(vmem_limit_bytes=60 * MIB),
    )(send_list[0].T, p_tiles)
    arrived = lax.all_to_all(
        outgoing.reshape(peers, slots, HALF, LANES), ("px", "py"), split_axis=0, concat_axis=0, tiled=True
    ).reshape(peers * slots, HALF, LANES)

    sums = coarse_here * PS
    room = groups * LIST + STAGE
    local, tiles, meta, count = pl.pallas_call(
        functools.partial(project_kernel, peers * slots),
        grid=(groups,),
        in_specs=[
            whole((per_row, rows)),
            whole((per_row, rows)),
            whole((1, rows)),
            pl.BlockSpec((per_row, 1, KROWS, LANES), lambda g: (0, g, 0, 0)),
            pl.BlockSpec((1, KROWS, LANES), lambda g: (g, 0, 0)),
            whole((rows, HALF, LANES)),
        ],
        out_specs=[whole((PIECES * sums, HALF, LANES)), hbm, smem, smem],
        out_shape=[
            jax.ShapeDtypeStruct((PIECES * sums, HALF, LANES), jnp.float32),
            jax.ShapeDtypeStruct((PIECES, room, B, LANES), bf16),
            jax.ShapeDtypeStruct((2 * PIECES, room), jnp.int32),
            jax.ShapeDtypeStruct((PIECES,), jnp.int32),
        ],
        scratch_shapes=[
            pltpu.VMEM((GROUP * B, 2 * KROWS), bf16),
            pltpu.VMEM((rows + 1, B, LANES), bf16),
            pltpu.VMEM((rows + 1, B, LANES), bf16),
            pltpu.VMEM((PIECES * sums, HALF, LANES), jnp.float32),
            pltpu.VMEM((PIECES * LIST, B, LANES), bf16),
            pltpu.VMEM((PIECES * LIST, B, LANES), bf16),
            pltpu.VMEM((PIECES, STAGE, B, LANES), bf16),
            pltpu.VMEM((2, per_row, rows), jnp.int32),
            pltpu.SMEM((2, per_row, rows), jnp.int32),
            pltpu.SMEM((2, PIECES * LIST), jnp.int32),
            pltpu.SMEM((PIECES,), jnp.int32),
            pltpu.SMEM((PIECES,), jnp.int32),
            pltpu.SemaphoreType.DMA,
            pltpu.SemaphoreType.DMA((PIECES, STAGE // CHUNK)),
        ],
        compiler_params=pltpu.CompilerParams(vmem_limit_bytes=63 * MIB),
        cost_estimate=pl.CostEstimate(
            flops=4 * 512 * 512 * 128 * pairs * groups, bytes_accessed=45_000_000, transcendentals=0
        ),
    )(a_source.T, coarse_slot.T, agg_local.reshape(1, rows), a_tiles, p_tiles, own)

    piece_rows = CCAP * PS * HALF + 16
    me = lax.axis_index("py").reshape(1)
    sent = pl.pallas_call(
        functools.partial(combine_kernel, 0, peers_y),
        in_specs=[smem, smem, smem, smem, hbm, hbm, hbm],
        out_specs=[hbm] * peers_y,
        out_shape=[jax.ShapeDtypeStruct((piece_rows, LANES), bf16)] * peers_y,
        scratch_shapes=[
            pltpu.VMEM((peers * slots + 1, HALF, LANES), bf16),
            pltpu.VMEM((sums + 1, HALF, LANES), jnp.float32),
            pltpu.VMEM((sums + 1, HALF, LANES), jnp.float32),
            pltpu.VMEM((RING, CHUNK, B, LANES), bf16),
            pltpu.VMEM((peers_y, piece_rows, LANES), bf16),
            pltpu.SMEM((coarse_here,), jnp.int32),
            pltpu.SMEM((peers_y * CCAP,), jnp.int32),
            pltpu.SMEM((peers_y,), jnp.int32),
            pltpu.SemaphoreType.DMA,
            pltpu.SemaphoreType.DMA,
            pltpu.SemaphoreType.DMA((peers_y,)),
            pltpu.SemaphoreType.DMA((RING,)),
            pltpu.SemaphoreType.DMA((coarse_here,)),
        ],
        compiler_params=pltpu.CompilerParams(vmem_limit_bytes=56 * MIB),
        cost_estimate=pl.CostEstimate(flops=4_000_000_000, bytes_accessed=8_000_000, transcendentals=0),
    )(meta, count, coarse_target, me, arrived, local, tiles)
    received = [sent[0]]
    for d in range(1, peers_y):
        received.append(lax.ppermute(sent[d], "py", [(i, i ^ d) for i in range(peers_y)]))

    per_step = 9
    out_groups = coarse_here // GROUP
    placed = pl.pallas_call(
        functools.partial(place_kernel, peers_y),
        grid=(S // per_step,),
        in_specs=[hbm] * peers_y,
        out_specs=pl.BlockSpec((per_step, out_groups, KROWS, LANES), lambda s: (s, 0, 0, 0)),
        out_shape=jax.ShapeDtypeStruct((S, out_groups, KROWS, LANES), bf16),
        scratch_shapes=[
            pltpu.VMEM((peers_y, piece_rows, LANES), bf16),
            pltpu.SMEM((coarse_here + 1,), jnp.int32),
            pltpu.SMEM((coarse_here + 1,), jnp.int32),
            pltpu.SemaphoreType.DMA((peers_y,)),
        ],
        compiler_params=pltpu.CompilerParams(vmem_limit_bytes=24 * MIB),
        cost_estimate=pl.CostEstimate(flops=1_000_000_000, bytes_accessed=3_000_000, transcendentals=0),
    )(*received)
    return from_tiles(placed).transpose(1, 0, 2)


def solution(mesh):
    rows = ("px", "py")
    in_specs = (
        P(rows, None, None),
        P(rows, None),
        P(rows, None),
        P(rows, None, None),
        P(rows),
        P(rows, None),
        P(rows),
    )
    return jax.shard_map(body, mesh=mesh, in_specs=in_specs, out_specs=P(rows, None, None), check_vma=False)
```

```python
import functools

import jax
import jax.numpy as jnp
from jax import lax
from jax.experimental import pallas as pl
from jax.experimental.pallas import tpu as pltpu
from jax.sharding import PartitionSpec as P

B = 64
FLAT = B * B
LANES = 128
HALF = B // 2
S = 27
AGG = 6
CCAP = 2
GROUP = 8
TILES = FLAT // LANES
KROWS = GROUP * TILES
PIECES = 2
CHUNK = 32
PEERS = 8
TURN = 8
LIST = 128
STAGE = LIST + 2 * CHUNK
SRC_BITS = 7
PLACE_BITS = 10
FLAG_BIT = 30
RING = 4
MIB = 1 << 20


def lane_low(rows):
    return lax.broadcasted_iota(jnp.int32, (rows, LANES), 1) < B


def swap_halves(x):
    return pltpu.roll(x, B, 1)


def as_tiles(x):
    lead, rows = x.shape[:-2], x.shape[-2]
    split = x.reshape(*lead, rows // GROUP, GROUP, TILES, LANES)
    return jnp.swapaxes(split, -3, -2).reshape(*lead, rows // GROUP, KROWS, LANES)


def from_tiles(x):
    lead, groups = x.shape[:-3], x.shape[-3]
    split = x.reshape(*lead, groups, TILES, GROUP, LANES)
    return jnp.swapaxes(split, -3, -2).reshape(*lead, groups * GROUP, FLAT)


def block_perm(transposed):
    block_axis, tile_axis = (1, 0) if transposed else (0, 1)
    shape = (KROWS, KROWS)
    block_row = lax.broadcasted_iota(jnp.int32, shape, block_axis)
    tile_row = lax.broadcasted_iota(jnp.int32, shape, tile_axis)
    same_r = (block_row // HALF) == (tile_row % GROUP)
    want = 2 * ((tile_row % LANES) // GROUP) + tile_row // LANES
    same_j = (block_row % HALF) == want
    return jnp.where(same_r & same_j, 1.0, 0.0).astype(jnp.bfloat16)


def pack_kernel(
    send_hbm, p_hbm, out_hbm, own_hbm, send_ref, p_ref, table_ref, out_ref, sems, send_sem, own_sem, out_sems
):
    groups = p_ref.shape[0]
    rows = groups * GROUP
    slots, peers = send_ref.shape
    get_send = pltpu.make_async_copy(send_hbm, send_ref, send_sem)
    get_send.start()

    def get(g):
        return pltpu.make_async_copy(p_hbm.at[pl.ds(g, 2)], p_ref.at[pl.ds(g, 2)], sems.at[g // 2])

    for g in range(0, groups, 2):
        get(g).start()
    perm = block_perm(False)
    low = lane_low(LANES)

    def to_blocks(g):
        top, bottom = p_ref[g, 0:LANES, :], p_ref[g, LANES:KROWS, :]
        even = jnp.where(low, top, swap_halves(bottom))
        odd = jnp.where(low, swap_halves(top), bottom)
        return jnp.concatenate([even, odd], axis=0)

    for g in range(0, groups, 2):
        get(g).wait()
        both = jnp.concatenate([to_blocks(g), to_blocks(g + 1)], axis=1)
        blocks = jnp.dot(perm, both, preferred_element_type=jnp.float32).astype(jnp.bfloat16)
        for h in range(2):
            piece = blocks[:, h * LANES : (h + 1) * LANES].reshape(GROUP, HALF, LANES)
            table_ref[pl.ds((g + h) * GROUP, GROUP)] = piece
    put_own = pltpu.make_async_copy(table_ref.at[pl.ds(0, rows)], own_hbm, own_sem)
    put_own.start()
    table_ref[rows] = jnp.zeros((HALF, LANES), jnp.bfloat16)
    get_send.wait()

    def fill(peer, carry):
        for slot in range(slots):
            wanted = send_ref[slot, peer]
            out_ref[peer * slots + slot] = table_ref[jnp.where(wanted < 0, rows, wanted)]
        return carry

    def put(i):
        span = pl.ds(i * PEERS * slots, PEERS * slots)
        return pltpu.make_async_copy(out_ref.at[span], out_hbm.at[span], out_sems.at[i])

    for i in range(peers // PEERS):
        lax.fori_loop(i * PEERS, (i + 1) * PEERS, fill, 0, unroll=2)
        put(i).start()
    put_own.wait()
    for i in range(peers // PEERS):
        put(i).wait()


def fold(value, low):
    top, bottom = value[0:HALF], value[HALF:]
    return jnp.where(low, top, swap_halves(bottom)), jnp.where(low, swap_halves(top), bottom)


def project_kernel(
    ghosts, peers, target_ref, me_ref, source_ref, slot_ref, agg_ref, a_ref, p_ref, own_ref, sum_ref, tiles_hbm, meta_ref, count_ref,
    left_ref, first_ref, second_ref, odd_ref, even_tiles, odd_tiles, stage_ref,
    words_vec, words_ref, here_ref, done_ref, flying_ref, words_sem, sems,
):
    step = pl.program_id(0)
    last = pl.num_programs(0) - 1
    per_row, rows = source_ref.shape
    pairs = (per_row + 3) // 4 * 2
    sums = sum_ref.shape[0]
    low_half, low_all = lane_low(HALF), lane_low(B)
    zero_all = jnp.zeros((B, LANES), jnp.bfloat16)

    @pl.when(step == 0)
    def _():
        source, slot = source_ref[...], slot_ref[...]
        coarse_here = target_ref.shape[0]
        agg = agg_ref[...]
        near = jnp.zeros_like(agg)
        for c in range(coarse_here):
            peer = lax.rem(lax.div(target_ref[c], coarse_here), peers)
            near = jnp.where(agg == c, ((peer ^ me_ref[0]) < peers // 2).astype(jnp.int32), near)
        place = agg * S + slot
        ghost = (source >= rows).astype(jnp.int32)
        words_vec[0] = (place << SRC_BITS) + jnp.minimum(source, rows)
        words_vec[1] = (ghost << FLAG_BIT) + (near << FLAG_BIT - 1) + (jnp.maximum(source - rows, 0) << PLACE_BITS) + place
        load = pltpu.make_async_copy(words_vec, words_ref, words_sem)
        load.start()
        for i in range(PIECES):
            done_ref[i] = 0
            flying_ref[i] = 0

        def expand(i, carry):
            block = own_ref[i]
            turned = swap_halves(block)
            zero = jnp.zeros((HALF, LANES), jnp.bfloat16)
            first_ref[i, 0:HALF] = jnp.where(low_half, block, zero)
            first_ref[i, HALF:] = jnp.where(low_half, turned, zero)
            second_ref[i, 0:HALF] = jnp.where(low_half, zero, turned)
            second_ref[i, HALF:] = jnp.where(low_half, zero, block)
            return carry

        lax.fori_loop(0, rows, expand, 0, unroll=8)
        first_ref[rows] = zero_all
        second_ref[rows] = zero_all

        def clear(i, carry):
            sum_ref[i] = jnp.zeros((HALF, LANES), jnp.float32)
            odd_ref[i] = jnp.zeros((HALF, LANES), jnp.float32)
            return carry

        lax.fori_loop(0, sums, clear, 0, unroll=4)
        load.wait()

    flipped = p_ref[0].T
    row_of = lax.broadcasted_iota(jnp.int32, (B, KROWS), 1) % GROUP
    zero = jnp.zeros((B, KROWS), jnp.bfloat16)
    for r in range(GROUP):
        mine = row_of == r
        left_ref[r * B : (r + 1) * B, 0:KROWS] = jnp.where(mine, flipped[0:B], zero)
        left_ref[r * B : (r + 1) * B, KROWS:] = jnp.where(mine, flipped[B:], zero)
    low = lane_low(KROWS)

    def pair_of(pair):
        first = a_ref[2 * pair, 0]
        second = a_ref[min(2 * pair + 1, per_row - 1), 0]
        even = jnp.where(low, first, swap_halves(second))
        odd = jnp.where(low, swap_halves(first), second)
        return jnp.concatenate([even, odd], axis=0)

    counts = [jnp.int32(0), jnp.int32(0)]
    for pair in range(0, pairs, 2):
        right = jnp.concatenate([pair_of(pair), pair_of(pair + 1)], axis=1)
        both = jnp.dot(left_ref[...], right, preferred_element_type=jnp.float32).astype(jnp.bfloat16)
        for r in range(GROUP):
            row = step * GROUP + r
            moving = both[r * B : (r + 1) * B]
            for h in range(2):
                tile = moving[:, h * LANES : (h + 1) * LANES]
                halves, targets = [], []
                for parity, table, listed in ((0, first_ref, even_tiles), (1, second_ref, odd_tiles)):
                    k = 2 * (pair + h) + parity
                    if k >= per_row:
                        halves.append(zero_all)
                        targets.append(None)
                        continue
                    word = words_ref[0, k, row]
                    halves.append(table[word & ((1 << SRC_BITS) - 1)])
                    targets.append(word >> SRC_BITS)
                    if k > 0:
                        note = words_ref[1, k, row]
                        shift = (note >> FLAG_BIT - 4) & 8
                        at = ((counts[parity] >> shift) & (LIST - 1)) + (shift << 4)
                        listed[at] = tile
                        here_ref[parity, at] = note
                        counts[parity] += (note >> FLAG_BIT) << shift
                filled = jnp.concatenate(halves, axis=0)
                value = jnp.dot(tile, filled, preferred_element_type=jnp.float32)
                even, odd = fold(value, low_half)
                sum_ref[targets[0]] += even
                if targets[1] is not None:
                    odd_ref[targets[1]] += odd

    no_entry = (ghosts << PLACE_BITS) + sums
    for part in range(PIECES):
        even_count = (counts[0] >> 8 * part) & (LIST - 1)
        odd_count = (counts[1] >> 8 * part) & (LIST - 1)
        after = jnp.maximum(even_count, odd_count)
        before = done_ref[part]
        chunks = lax.div(after + CHUNK - 1, CHUNK) + jnp.where(step == last, 1, 0)

        def copy(i, start, part=part):
            return pltpu.make_async_copy(
                stage_ref.at[part, pl.ds(i * CHUNK, CHUNK)],
                tiles_hbm.at[part, pl.ds(start + i * CHUNK, CHUNK)],
                sems.at[part, i],
            )

        def finish(i, carry, copy=copy):
            copy(i, 0).wait()
            return carry

        lax.fori_loop(0, flying_ref[part], finish, 0)

        def merge(turn, carry, part=part, even_count=even_count, odd_count=odd_count, before=before):
            for j in range(TURN):
                i = turn * TURN + j
                end = part * LIST + jnp.minimum(i, LIST - 1)
                even_at = jnp.where(low_all, i, STAGE) < even_count
                odd_at = jnp.where(low_all, STAGE, i) < odd_count
                tile = jnp.where(even_at, even_tiles[end], zero_all)
                stage_ref[part, i] = jnp.where(odd_at, odd_tiles[end], tile)
                meta_ref[2 * part, before + i] = jnp.where(i < even_count, here_ref[0, end], no_entry)
                meta_ref[2 * part + 1, before + i] = jnp.where(i < odd_count, here_ref[1, end], no_entry)
            return carry

        turns = jnp.where(step == last, chunks * (CHUNK // TURN), (after + TURN - 1) >> 3)
        lax.fori_loop(0, turns, merge, 0)

        def send(i, carry, copy=copy, before=before):
            copy(i, before).start()
            return carry

        lax.fori_loop(0, chunks, send, 0)
        flying_ref[part] = chunks
        done_ref[part] = before + after

    @pl.when(step == last)
    def _():
        def total(i, carry):
            sum_ref[i] += odd_ref[i]
            return carry

        lax.fori_loop(0, sums, total, 0, unroll=4)
        for part in range(PIECES):
            count_ref[part] = lax.div(done_ref[part] + CHUNK - 1, CHUNK)

            def drain(i, carry, part=part):
                pltpu.make_async_copy(
                    stage_ref.at[part, pl.ds(i * CHUNK, CHUNK)],
                    tiles_hbm.at[part, pl.ds(i * CHUNK, CHUNK)],
                    sems.at[part, i],
                ).wait()
                return carry

            lax.fori_loop(0, flying_ref[part], drain, 0)


def offsets_of(part, peers):
    return range(peers // 2, peers) if part == 0 else range(peers // 2)


def combine_kernel(
    part, peers, meta_ref, count_ref, target_ref, me_ref, ghost_hbm, sum_hbm, tiles_hbm, *rest
):
    mine = offsets_of(part, peers)
    outs = dict(zip(mine, rest))
    (
        ghost_ref, even_ref, odd_ref, tiles_ref, out_ref, bucket_ref, place_ref, per_peer_ref,
        ghost_sem, sum_sem, note_sems, sems, out_sems,
    ) = rest[len(mine) :]
    me = me_ref[0]
    ghosts = ghost_hbm.shape[0]
    coarse_here = target_ref.shape[0]
    sums = coarse_here * S
    chunks = count_ref[part]
    low_half = lane_low(HALF)
    zero_half = jnp.zeros((HALF, LANES), jnp.bfloat16)
    load_sums = pltpu.make_async_copy(sum_hbm, even_ref.at[pl.ds(0, sums)], sum_sem)
    load_sums.start()
    load_ghosts = pltpu.make_async_copy(ghost_hbm, ghost_ref.at[pl.ds(0, ghosts)], ghost_sem)
    load_ghosts.start()

    def fetch(i):
        slot = lax.rem(i, RING)
        return pltpu.make_async_copy(tiles_hbm.at[part, pl.ds(i * CHUNK, CHUNK)], tiles_ref.at[slot], sems.at[slot])

    for i in range(RING - 1):

        @pl.when(i < chunks)
        def _():
            fetch(i).start()

    ghost_ref[ghosts] = zero_half

    def clear(i, carry):
        odd_ref[i] = jnp.zeros((HALF, LANES), jnp.float32)
        return carry

    lax.fori_loop(0, sums, clear, 0, unroll=8)

    for p in range(peers):
        per_peer_ref[p] = 0
        for q in range(CCAP):
            place_ref[p * CCAP + q] = -1

    def assign(c, carry):
        target = target_ref[c]
        peer = lax.rem(lax.div(target, coarse_here), peers)
        bucket = peer * CCAP + per_peer_ref[peer]
        per_peer_ref[peer] = per_peer_ref[peer] + 1
        bucket_ref[c] = bucket
        place_ref[bucket] = lax.rem(target, coarse_here)
        return carry

    lax.fori_loop(0, coarse_here, assign, 0)
    payload = CCAP * S * HALF
    second_slot = lax.broadcasted_iota(jnp.int32, (out_ref.shape[1] - payload, LANES), 1) // HALF % CCAP

    def note(p, carry):
        value = jnp.full(second_slot.shape, -1, jnp.int32)
        for q in range(CCAP):
            value = jnp.where(second_slot == q, place_ref[(p ^ me) * CCAP + q], value)
        out_ref[p, payload:] = value.astype(jnp.float32).astype(jnp.bfloat16)
        return carry

    lax.fori_loop(0, peers, note, 0)
    notes = pl.ds(payload, out_ref.shape[1] - payload)

    def put_notes(d):
        return pltpu.make_async_copy(out_ref.at[d, notes], outs[d].at[notes], note_sems.at[d])

    for d in mine:
        put_notes(d).start()
    load_ghosts.wait()
    load_sums.wait()

    def work(i, carry):
        @pl.when(i + RING - 1 < chunks)
        def _():
            fetch(i + RING - 1).start()

        fetch(i).wait()
        slot = lax.rem(i, RING)
        for j in range(CHUNK):
            at = i * CHUNK + j
            even, odd = meta_ref[2 * part, at], meta_ref[2 * part + 1, at]
            first = ghost_ref[(even >> PLACE_BITS) & ((1 << FLAG_BIT - PLACE_BITS - 1) - 1)]
            second = ghost_ref[(odd >> PLACE_BITS) & ((1 << FLAG_BIT - PLACE_BITS - 1) - 1)]
            filled = jnp.concatenate(
                [
                    jnp.where(low_half, first, zero_half),
                    jnp.where(low_half, swap_halves(first), zero_half),
                    jnp.where(low_half, zero_half, swap_halves(second)),
                    jnp.where(low_half, zero_half, second),
                ],
                axis=0,
            )
            value = jnp.dot(tiles_ref[slot, j], filled, preferred_element_type=jnp.float32)
            to_even, to_odd = fold(value, low_half)
            even_ref[even & ((1 << PLACE_BITS) - 1)] += to_even
            odd_ref[odd & ((1 << PLACE_BITS) - 1)] += to_odd
        return carry

    lax.fori_loop(0, chunks, work, 0)

    def put(c, d, start):
        span = pl.ds(start, S * HALF)
        return pltpu.make_async_copy(out_ref.at[d, span], outs[d].at[span], out_sems.at[c])

    def finish(c, carry):
        bucket = bucket_ref[c]
        start = pl.multiple_of(lax.rem(bucket, CCAP) * (S * HALF), HALF)
        offset = lax.div(bucket, CCAP) ^ me
        first = c * S

        @pl.when((offset >= mine[0]) & (offset <= mine[-1]))
        def _():
            for s in range(S):
                total = even_ref[first + s] + odd_ref[first + s]
                out_ref[offset, pl.ds(pl.multiple_of(start + s * HALF, HALF), HALF)] = total.astype(jnp.bfloat16)

        for d in mine:

            @pl.when(offset == d)
            def _():
                put(c, d, start).start()

        return carry

    lax.fori_loop(0, coarse_here, finish, 0)
    for d in mine:
        put_notes(d).wait()

    def drain(c, carry):
        offset = lax.div(bucket_ref[c], CCAP) ^ me

        @pl.when((offset >= mine[0]) & (offset <= mine[-1]))
        def _():
            put(c, mine[0], 0).wait()

        return carry

    lax.fori_loop(0, coarse_here, drain, 0)


def place_kernel(peers, *refs):
    parts = refs[:peers]
    out_ref, in_ref, peer_ref, start_ref, sems = refs[peers:]
    step = pl.program_id(0)
    per_step, groups = out_ref.shape[0], out_ref.shape[1]
    payload = CCAP * S * HALF

    @pl.when(step == 0)
    def _():
        loads = [pltpu.make_async_copy(parts[d], in_ref.at[d], sems.at[d]) for d in range(peers)]
        for load in loads:
            load.start()
        for load in loads:
            load.wait()
        for p in range(peers):
            notes = in_ref[p, payload:].astype(jnp.float32)
            which = lax.broadcasted_iota(jnp.int32, notes.shape, 1) // HALF
            for q in range(CCAP):
                place = jnp.max(jnp.where(which == q, notes, -1.0)).astype(jnp.int32)
                entry = jnp.where(place < 0, groups * GROUP, place)
                peer_ref[entry] = p
                start_ref[entry] = q * S * HALF

    perm = block_perm(True)
    low = lane_low(LANES)
    for i in range(per_step):
        s = step * per_step + i
        columns = []
        for g in range(groups):
            blocks = []
            for c in range(GROUP):
                row = g * GROUP + c
                here = pl.multiple_of(start_ref[row] + s * HALF, HALF)
                blocks.append(in_ref[peer_ref[row], pl.ds(here, HALF)])
            columns.append(jnp.concatenate(blocks, axis=0))
        moved = jnp.dot(perm, jnp.concatenate(columns, axis=1), preferred_element_type=jnp.float32)
        moved = moved.astype(jnp.bfloat16)
        for g in range(groups):
            mine = moved[:, g * LANES : (g + 1) * LANES]
            even, odd = mine[0:LANES], mine[LANES:]
            out_ref[i, g, 0:LANES] = jnp.where(low, even, swap_halves(odd))
            out_ref[i, g, LANES:] = jnp.where(low, swap_halves(even), odd)


def whole(shape):
    return pl.BlockSpec(shape, lambda *_: (0,) * len(shape))


def body(a_blocks, p_blocks, a_source, send_list, agg_local, coarse_slot, coarse_target):
    rows, per_row, _ = a_blocks.shape
    peers = lax.axis_size(("px", "py"))
    peers_y = lax.axis_size("py")
    slots = send_list.shape[2]
    coarse_here = rows // AGG
    groups = rows // GROUP
    pairs = (per_row + 3) // 4 * 2
    bf16 = jnp.bfloat16
    smem = pl.BlockSpec(memory_space=pltpu.SMEM)

    a_tiles = as_tiles(a_blocks.transpose(1, 0, 2))
    p_tiles = as_tiles(p_blocks)
    hbm = pl.BlockSpec(memory_space=pltpu.HBM)
    outgoing, own = pl.pallas_call(
        pack_kernel,
        in_specs=[hbm, hbm],
        out_specs=[hbm, hbm],
        out_shape=[
            jax.ShapeDtypeStruct((peers * slots, HALF, LANES), bf16),
            jax.ShapeDtypeStruct((rows, HALF, LANES), bf16),
        ],
        scratch_shapes=[
            pltpu.SMEM((slots, peers), jnp.int32),
            pltpu.VMEM((groups, KROWS, LANES), bf16),
            pltpu.VMEM((rows + 1, HALF, LANES), bf16),
            pltpu.VMEM((peers * slots, HALF, LANES), bf16),
            pltpu.SemaphoreType.DMA((groups // 2,)),
            pltpu.SemaphoreType.DMA,
            pltpu.SemaphoreType.DMA,
            pltpu.SemaphoreType.DMA((peers // PEERS,)),
        ],
        compiler_params=pltpu.CompilerParams(vmem_limit_bytes=60 * MIB),
    )(send_list[0].T, p_tiles)
    arrived = lax.all_to_all(
        outgoing.reshape(peers, slots, HALF, LANES), ("px", "py"), split_axis=0, concat_axis=0, tiled=True
    ).reshape(peers * slots, HALF, LANES)

    me = lax.axis_index("py").reshape(1)
    sums = coarse_here * S
    room = groups * LIST + STAGE
    local, tiles, meta, count = pl.pallas_call(
        functools.partial(project_kernel, peers * slots, peers_y),
        grid=(groups,),
        in_specs=[
            smem,
            smem,
            whole((per_row, rows)),
            whole((per_row, rows)),
            whole((1, rows)),
            pl.BlockSpec((per_row, 1, KROWS, LANES), lambda g: (0, g, 0, 0)),
            pl.BlockSpec((1, KROWS, LANES), lambda g: (g, 0, 0)),
            whole((rows, HALF, LANES)),
        ],
        out_specs=[whole((sums, HALF, LANES)), hbm, smem, smem],
        out_shape=[
            jax.ShapeDtypeStruct((sums, HALF, LANES), jnp.float32),
            jax.ShapeDtypeStruct((PIECES, room, B, LANES), bf16),
            jax.ShapeDtypeStruct((2 * PIECES, room), jnp.int32),
            jax.ShapeDtypeStruct((PIECES,), jnp.int32),
        ],
        scratch_shapes=[
            pltpu.VMEM((GROUP * B, 2 * KROWS), bf16),
            pltpu.VMEM((rows + 1, B, LANES), bf16),
            pltpu.VMEM((rows + 1, B, LANES), bf16),
            pltpu.VMEM((sums, HALF, LANES), jnp.float32),
            pltpu.VMEM((PIECES * LIST, B, LANES), bf16),
            pltpu.VMEM((PIECES * LIST, B, LANES), bf16),
            pltpu.VMEM((PIECES, STAGE, B, LANES), bf16),
            pltpu.VMEM((2, per_row, rows), jnp.int32),
            pltpu.SMEM((2, per_row, rows), jnp.int32),
            pltpu.SMEM((2, PIECES * LIST), jnp.int32),
            pltpu.SMEM((PIECES,), jnp.int32),
            pltpu.SMEM((PIECES,), jnp.int32),
            pltpu.SemaphoreType.DMA,
            pltpu.SemaphoreType.DMA((PIECES, STAGE // CHUNK)),
        ],
        compiler_params=pltpu.CompilerParams(vmem_limit_bytes=63 * MIB),
        cost_estimate=pl.CostEstimate(
            flops=4 * 512 * 512 * 128 * pairs * groups, bytes_accessed=45_000_000, transcendentals=0
        ),
    )(coarse_target, me, a_source.T, coarse_slot.T, agg_local.reshape(1, rows), a_tiles, p_tiles, own)

    piece_rows = CCAP * S * HALF + 16
    received = [None] * peers_y
    for part in range(PIECES):
        sent = pl.pallas_call(
            functools.partial(combine_kernel, part, peers_y),
            in_specs=[smem, smem, smem, smem, hbm, hbm, hbm],
            out_specs=[hbm] * len(offsets_of(part, peers_y)),
            out_shape=[jax.ShapeDtypeStruct((piece_rows, LANES), bf16)] * len(offsets_of(part, peers_y)),
            scratch_shapes=[
                pltpu.VMEM((peers * slots + 1, HALF, LANES), bf16),
                pltpu.VMEM((sums + 1, HALF, LANES), jnp.float32),
                pltpu.VMEM((sums + 1, HALF, LANES), jnp.float32),
                pltpu.VMEM((RING, CHUNK, B, LANES), bf16),
                pltpu.VMEM((peers_y, piece_rows, LANES), bf16),
                pltpu.SMEM((coarse_here,), jnp.int32),
                pltpu.SMEM((peers_y * CCAP,), jnp.int32),
                pltpu.SMEM((peers_y,), jnp.int32),
                pltpu.SemaphoreType.DMA,
                pltpu.SemaphoreType.DMA,
                pltpu.SemaphoreType.DMA((peers_y,)),
                pltpu.SemaphoreType.DMA((RING,)),
                pltpu.SemaphoreType.DMA((coarse_here,)),
            ],
            compiler_params=pltpu.CompilerParams(vmem_limit_bytes=56 * MIB),
            cost_estimate=pl.CostEstimate(flops=4_000_000_000, bytes_accessed=8_000_000, transcendentals=0),
        )(meta, count, coarse_target, me, arrived, local, tiles)
        for d, rows_out in zip(offsets_of(part, peers_y), sent):
            pairs_of = [(i, i ^ d) for i in range(peers_y)]
            received[d] = lax.ppermute(rows_out, "py", pairs_of) if d else rows_out

    per_step = 9
    out_groups = coarse_here // GROUP
    placed = pl.pallas_call(
        functools.partial(place_kernel, peers_y),
        grid=(S // per_step,),
        in_specs=[hbm] * peers_y,
        out_specs=pl.BlockSpec((per_step, out_groups, KROWS, LANES), lambda s: (s, 0, 0, 0)),
        out_shape=jax.ShapeDtypeStruct((S, out_groups, KROWS, LANES), bf16),
        scratch_shapes=[
            pltpu.VMEM((peers_y, piece_rows, LANES), bf16),
            pltpu.SMEM((coarse_here + 1,), jnp.int32),
            pltpu.SMEM((coarse_here + 1,), jnp.int32),
            pltpu.SemaphoreType.DMA((peers_y,)),
        ],
        compiler_params=pltpu.CompilerParams(vmem_limit_bytes=60 * MIB),
        cost_estimate=pl.CostEstimate(flops=1_000_000_000, bytes_accessed=3_000_000, transcendentals=0),
    )(*received)
    return from_tiles(placed).transpose(1, 0, 2)


def solution(mesh):
    rows = ("px", "py")
    in_specs = (
        P(rows, None, None),
        P(rows, None),
        P(rows, None),
        P(rows, None, None),
        P(rows),
        P(rows, None),
        P(rows),
    )
    return jax.shard_map(body, mesh=mesh, in_specs=in_specs, out_specs=P(rows, None, None), check_vma=False)
```
